256 devices in a mesh: wide: 16 (over x_hi, z), narrow: 16 (over x_lo, y, core).
Axes of the slice: x: 4 (x_hi: 2, x_lo: 2; x = x_hi * 2 + x_lo), y: 4, z: 8, core: 2. Of those that a mesh axis runs over, the one named last changes fastest.
Arguments:
- pair_act: bfloat16 [768, 768, 128], P('wide', 'narrow'), may hold values from -6 to 6
- residue_mask: int32 [768], replicated, may hold values 0 or 1
- w_proj_start: bfloat16 [128, 512], replicated, may hold values from -0.5 to 0.5
- w_bias_start: bfloat16 [128, 4], replicated, may hold values from -40 to 40
- w_out_start: bfloat16 [128, 128], replicated, may hold values from -0.5 to 0.5
- w_proj_end: bfloat16 [128, 512], replicated, may hold values from -0.5 to 0.5
- w_bias_end: bfloat16 [128, 4], replicated, may hold values from -40 to 40
- w_out_end: bfloat16 [128, 128], replicated, may hold values from -0.5 to 0.5
Outputs:
- update_start: bfloat16 [768, 768, 128], P('wide', 'narrow')
- update_end: bfloat16 [768, 768, 128], P('wide', 'narrow')
The draws below stay inside these ranges and needn't reach their ends.
All inputs are finite; a program needn't handle non-finite values.
Results may differ from the reference program's by a relative error of at most 0.012.
The reference program's roundings to bfloat16 on the way count: a program that leaves them out, or rounds other values in their place, can miss the bound.
Values may be sent and summed in bfloat16 or wider, within the bound.
A program may use at most 64 MiB of HBM per device.

```python
import jax
import jax.numpy as jnp
from jax import lax

N = 768
C = 128
HEADS = 4
HEAD_DIM = 32


def bias_columns(key, salt):
    key = jax.random.fold_in(key, salt)
    first_key = jax.random.fold_in(key, 0)
    third_key = jax.random.fold_in(key, 2)
    base = jax.random.truncated_normal(first_key, -4.0, 4.0, (C, HEADS), jnp.float32) * 128.0 ** (-0.5)
    factors = jax.random.uniform(third_key, (HEADS,), jnp.float32, 0.5, 2.0)
    return (base * factors[None, :]).astype(jnp.bfloat16)


def draw_w_bias_start(key, part):
    return bias_columns(key, 1701)


def draw_w_bias_end(key, part):
    return bias_columns(key, 2903)


def plant(drawn, own_key, smallest, top_value):
    spot = [jax.random.randint(jax.random.fold_in(own_key, axis), (), 0, length) for axis, length in enumerate(drawn.shape)]
    widest = drawn.shape.index(max(drawn.shape))
    next_to = spot[:widest] + [(spot[widest] + 1) % drawn.shape[widest]] + spot[widest + 1:]
    return drawn.at[tuple(spot)].set(smallest).at[tuple(next_to)].set(top_value)


def shard_levels(own_key, extent, shards, low, high):
    level = 1.0
    for axis_at, parts in shards:
        heights = jax.random.uniform(jax.random.fold_in(jax.random.fold_in(own_key, 6), axis_at), (parts,), jnp.float32, low / len(shards), high / len(shards))
        level = level * jnp.repeat(jnp.exp(heights), extent[axis_at] // parts).reshape((-1,) + (1,) * (len(extent) - 1 - axis_at))
    return level


def bell_draw(key, extent, scale, reach, cuts=(), held_as=jnp.bfloat16):
    array = scale * jax.random.normal(key, extent, jnp.float32)
    if cuts:
        array = array * shard_levels(key, extent, cuts, -0.22, 0.18)
    return jnp.clip(array, -reach, reach).astype(held_as)


def setup_inputs(seed: int = 0) -> dict:
    arg_keys = jax.random.split(jax.random.key(seed), 9)
    return {
        "pair_act": bell_draw(arg_keys[0], (N, N, C), 1.0, 6.0, ((0, 16), (1, 16))),
        "residue_mask": plant((jax.random.randint(arg_keys[1], (N,), 0, 8) < 7).astype(jnp.int32), jax.random.fold_in(arg_keys[1], 1), 0, 1),
        "w_proj_start": bell_draw(arg_keys[2], (C, HEADS * 4 * HEAD_DIM), C ** -0.5, 0.5),
        "w_bias_start": draw_w_bias_start(jax.random.fold_in(arg_keys[8], 71), 0),
        "w_out_start": bell_draw(arg_keys[4], (HEADS * HEAD_DIM, C), (HEADS * HEAD_DIM) ** -0.5, 0.5),
        "w_proj_end": bell_draw(arg_keys[5], (C, HEADS * 4 * HEAD_DIM), C ** -0.5, 0.5),
        "w_bias_end": draw_w_bias_end(jax.random.fold_in(arg_keys[8], 71), 0),
        "w_out_end": bell_draw(arg_keys[7], (HEADS * HEAD_DIM, C), (HEADS * HEAD_DIM) ** -0.5, 0.5),
    }


norm_eps = 1e-05
masked_score = -1000000000.0

def layer_norm(features):
    average = lax.optimization_barrier(jnp.mean(features, axis=-1, keepdims=True))
    centred = features - average
    spread = lax.optimization_barrier(jnp.mean(centred * centred, axis=-1, keepdims=True))
    return (centred * lax.rsqrt(spread + norm_eps)).astype(jnp.bfloat16)

def attend(projected, pair_bias, row_ok, key_ok):
    inv_root = HEAD_DIM ** (-0.5)

    def one_row(item_pair):
        packed, valid_row = item_pair
        packed = packed.reshape(N, HEADS, 4, HEAD_DIM).astype(jnp.float32)
        queries = packed[:, :, 0]
        keyset = packed[:, :, 1]
        values = packed[:, :, 2]
        gating = packed[:, :, 3]
        scores = jnp.einsum('bhd,khd->hbk', queries, keyset) * inv_root + pair_bias
        allowed = jnp.logical_and(valid_row, key_ok)
        scores = jnp.where(allowed[None, None, :], scores, masked_score)
        weights = jax.nn.softmax(scores, axis=-1).astype(jnp.bfloat16).astype(jnp.float32)
        summed = jnp.einsum('hbk,khd->bhd', weights, values)
        gated = (jax.nn.sigmoid(gating) * summed).astype(jnp.bfloat16)
        return gated.reshape(N, HEADS * HEAD_DIM)
    return lax.map(one_row, (projected, row_ok))

def start_node(features, residue_ok, w_proj, w_bias, w_out):
    normed = layer_norm(features)
    projected = jnp.dot(normed.reshape(N * N, C), w_proj, preferred_element_type=jnp.float32)
    projected = projected.astype(jnp.bfloat16).reshape(N, N, HEADS * 4 * HEAD_DIM)
    pair_bias = jnp.einsum('abc,ch->hab', normed.astype(jnp.float32), w_bias.astype(jnp.float32))
    gated = attend(projected, pair_bias, residue_ok, residue_ok)
    result = jnp.dot(gated.reshape(N * N, HEADS * HEAD_DIM), w_out, preferred_element_type=jnp.float32)
    return result.astype(jnp.bfloat16).reshape(N, N, C)

def reference(pair_act, residue_mask, w_proj_start, w_bias_start, w_out_start, w_proj_end, w_bias_end, w_out_end):
    residue_ok = residue_mask > 0
    update_start = start_node(pair_act.astype(jnp.float32), residue_ok, w_proj_start, w_bias_start, w_out_start)
    updated = pair_act.astype(jnp.float32) + update_start.astype(jnp.float32)
    flipped = jnp.transpose(updated, (1, 0, 2))
    update_end = start_node(flipped, residue_ok, w_proj_end, w_bias_end, w_out_end)
    update_end = jnp.transpose(update_end, (1, 0, 2))
    return (update_start, update_end)
```

```python
import functools
import math

import jax
import jax.numpy as jnp
import numpy as np
from jax import lax
from jax.experimental import pallas as pl
from jax.experimental.pallas import tpu as pltpu
from jax.sharding import Mesh
from jax.sharding import PartitionSpec as P

AXES = ("xh", "z", "xl", "y", "c")
SIZES = (2, 8, 2, 4, 2)
NARROW = ("xl", "y", "c")
WIDE = ("xh", "z")

HEADS = 4
DIM = 32
CH = HEADS * DIM
TILE = 48
N = 768
ROWS = 6
SUPER = 4
POS = 2 * TILE
EXP = POS * HEADS
SUB = 192
NORM_EPS = 1e-05
MASKED = -1000000000.0
INV_ROOT = DIM ** (-0.5)
ROOT = math.sqrt(DIM)
LOG2E = math.log2(math.e)
BF = jnp.bfloat16
F32 = jnp.float32


def layer_norm(features):
    average = jnp.mean(features, axis=-1, keepdims=True)
    centred = features - average
    spread = jnp.mean(centred * centred, axis=-1, keepdims=True)
    return (centred * lax.rsqrt(spread + NORM_EPS)).astype(BF)


def here():
    return {a: lax.axis_index(a) for a in AXES}


def place(at, **kw):
    return tuple(kw.get(a, at[a]) for a in AXES)


def dot(a, b, dims):
    return lax.dot_general(a, b, (dims, ((), ())), preferred_element_type=F32)


NN = ((1,), (0,))
NT = ((1,), (1,))


def send(src, dst, ssem, rsem, device):
    return pltpu.make_async_remote_copy(
        src_ref=src,
        dst_ref=dst,
        send_sem=ssem,
        recv_sem=rsem,
        device_id=device,
        device_id_type=pl.DeviceIdType.MESH,
    )


class Ring:
    def __init__(self, n, idx, whole, halves, plus, minus, ssem, rsem, base):
        self.n, self.idx = n, idx
        self.whole, self.halves = whole, halves
        self.plus, self.minus = plus, minus
        self.ssem, self.rsem, self.base = ssem, rsem, base
        self.sent = []

    def block(self, offset):
        return lax.rem(self.idx + offset + self.n, self.n)

    def copy(self, step, way, region):
        at = self.base + 2 * (step - 1) + way
        return send(region, region, self.ssem.at[at], self.rsem.at[at], self.minus if way else self.plus)

    def go(self, step, way, region):
        copy = self.copy(step, way, region)
        copy.start()
        self.sent.append(copy)

    def region(self, step, way, block):
        if 2 * step == self.n:
            return self.halves(block)[way]
        return self.whole(block)

    def start(self):
        for way in (0, 1):
            self.go(1, way, self.whole(self.idx))

    def advance(self, step):
        for way in (0, 1):
            came = self.block(step if way else -step)
            self.copy(step, way, self.region(step, way, came)).wait_recv()
            if 2 * step < self.n:
                self.go(step + 1, way, self.region(step + 1, way, came))

    def finish(self):
        for copy in self.sent:
            copy.wait_send()


def picker(offset, transposed):
    shape = (CH, 4 * CH) if transposed else (4 * CH, CH)
    d = lax.broadcasted_iota(jnp.int32, shape, 0 if transposed else 1)
    x = lax.broadcasted_iota(jnp.int32, shape, 1 if transposed else 0)
    return jnp.where(x == (d >> 5) * CH + offset * DIM + (d & 31), 1.0, 0.0).astype(BF)


def node_kernel(
    starting,
    tile_ref,
    mask_smem,
    key_ok_ref,
    w_proj_ref,
    w_bias_ref,
    w_out_ref,
    expand_ref,
    collapse_ref,
    head_ref,
    out_ref,
    nt,
    rows,
    bias,
    k_t,
    v_ext,
    q_exp,
    g_exp,
    gat,
    upd,
    ret,
    a_send,
    a_recv,
    f_send,
    f_recv,
    p_send,
    p_recv,
    g_send,
    g_recv,
    r_send,
    r_recv,
):
    at = here()
    xh, z, xl, y, c = (at[a] for a in AXES)
    x = 2 * xh + xl
    other = 1 - c
    if starting:
        n_peer, take = 8, 6
        me = xl * 4 + y
        peer_place = lambda j, core: place(at, xl=j // 4, y=lax.rem(j, 4), c=core)
        slot = lambda j, core: (2 * j + core, slice(None))
    else:
        n_peer, take = 16, 3
        me = xh * 8 + z
        peer_place = lambda j, core: place(at, xh=j // 8, z=lax.rem(j, 8), c=core)
        slot = lambda j, core: (j, pl.ds(3 * core, 3))

    def peer(d):
        return lax.rem(me + d, n_peer)

    def x_place(step):
        to = lax.rem(x + step + 4, 4)
        return place(at, xh=to // 2, xl=lax.rem(to, 2))

    y_place = lambda step: place(at, y=lax.rem(y + step + 4, 4))
    z_place = lambda step: place(at, z=lax.rem(z + step + 8, 8))
    sibling = place(at, c=other)

    partners = [peer_place(peer(d), c) for d in range(1, n_peer)]
    partners.append(sibling)
    if starting:
        partners += [z_place(d) for d in range(1, 8)]
        far = lax.rem(x + jnp.where(xl == 0, 3, 1), 4)
        partners.append(place(at, xh=far // 2, xl=lax.rem(far, 2)))
    else:
        partners += [peer_place(peer(d), other) for d in range(1, n_peer)]
        partners += [y_place(d) for d in range(1, 4)]
        partners += [x_place(1), x_place(-1)]
    barrier = pltpu.get_barrier_semaphore()
    for partner in partners:
        pl.semaphore_signal(barrier, inc=1, device_id=partner, device_id_type=pl.DeviceIdType.MESH)

    if starting:
        nt[...] = layer_norm(tile_ref[...].astype(F32))
        out_tile = nt
    else:
        out_tile = tile_ref
    own = out_tile[pl.ds(take * me, take)]
    rows[slot(me, c)] = own
    pl.semaphore_wait(barrier, len(partners))

    sends = []
    for d in range(1, n_peer):
        j = peer(d)
        copy = send(
            out_tile.at[pl.ds(take * j, take)],
            rows.at[slot(me, c)],
            a_send.at[d],
            a_recv.at[me],
            peer_place(j, c),
        )
        copy.start()
        sends.append(copy)

    def forward(d):
        j = peer(d)
        region = rows.at[slot(j, c)]
        copy = send(region, region, f_send.at[d], f_recv.at[j], sibling)
        copy.start()
        sends.append(copy)

    forward(0)

    w_all = w_proj_ref[...]
    w_kt = dot(picker(1, True), w_all, NT).astype(BF)
    w_v = dot(w_all, picker(2, False), NN).astype(BF)
    w_qg = jnp.concatenate([dot(w_all, picker(0, False), NN), dot(w_all, picker(3, False), NN)], axis=1).astype(BF)
    s_row = lax.broadcasted_iota(jnp.int32, (24, HEADS), 0)
    s_head = lax.broadcasted_iota(jnp.int32, (24, HEADS), 1)
    w_bias = w_bias_ref[...]
    w_rows = [
        dot(jnp.where(s_row == s_head * ROWS + r, 1.0, 0.0).astype(BF), w_bias, NT).astype(BF) for r in range(ROWS)
    ]

    for d in range(1, n_peer):
        j = peer(d)
        region = rows.at[slot(j, c)]
        send(region, region, a_send.at[d], a_recv.at[j], sibling).wait_recv()
        forward(d)
    for d in range(n_peer):
        j = peer(d)
        region = rows.at[slot(j, other)]
        send(region, region, f_send.at[d], f_recv.at[j], sibling).wait_recv()

    piece = jnp.zeros((24, N), F32)
    for r in range(ROWS):
        piece += dot(w_rows[r], rows[:, r].reshape(N, CH), NT)
    piece = jnp.where(key_ok_ref[...] > 0, piece * ROOT, MASKED)
    if starting:
        source = lax.rem(z, 2) == c
        z4 = z // 2
        own_piece = bias.at[xh, z4, xl, y]
    else:
        source = lax.rem(y, 2) == c
        y2 = y // 2
        own_piece = bias.at[xl, y2, xh, z]

    if starting:
        n_first, line, spot = 8, z, z_place
        part = lambda k: bias.at[xh, k, xl, y]
    else:
        n_first, line, spot = 4, y, y_place
        part = lambda k: bias.at[xl, k, xh, z]

    def first(d):
        return send(own_piece, own_piece, p_send.at[d], p_recv.at[line // 2], spot(d))

    @pl.when(source)
    def _():
        own_piece[...] = piece
        for d in range(1, n_first):
            first(d).start()

    for r in range(ROWS):
        x_r = rows[:, r].reshape(N, CH)
        k_t[r] = dot(w_kt, x_r, NT).astype(BF)
        v_ext[r, :, :CH] = dot(x_r, w_v, NN).astype(BF)
        v_ext[r, :, CH:] = jnp.ones((N, CH), BF)

    for k in range(n_first // 2):

        @pl.when(line != 2 * k + c)
        def _():
            send(part(k), part(k), p_send.at[0], p_recv.at[k], sibling).wait_recv()

    x_args = (x_place(1), x_place(-1), g_send, g_recv)
    if starting:
        y_args = (y_place(1), y_place(-1), g_send, g_recv)
        a1 = Ring(
            4, y, lambda k: bias.at[xh, pl.ds(0, 2), xl, k],
            lambda k: (bias.at[xh, 0, xl, k], bias.at[xh, 1, xl, k]), *y_args, 0,
        )
        b1 = Ring(
            4, x, lambda k: bias.at[k // 2, pl.ds(2, 2), lax.rem(k, 2), y],
            lambda k: (bias.at[k // 2, 2, lax.rem(k, 2), y], bias.at[k // 2, 3, lax.rem(k, 2), y]), *x_args, 8,
        )
        a2 = Ring(
            4, x, lambda k: bias.at[k // 2, pl.ds(0, 2), lax.rem(k, 2)],
            lambda k: (bias.at[k // 2, 0, lax.rem(k, 2)], bias.at[k // 2, 1, lax.rem(k, 2)]), *x_args, 16,
        )
        b2 = Ring(
            4, y, lambda k: bias.at[:, pl.ds(2, 2), :, k],
            lambda k: (bias.at[:, 2, :, k], bias.at[:, 3, :, k]), *y_args, 24,
        )
    else:
        z_args = (z_place(1), z_place(-1), g_send, g_recv)
        a1 = Ring(
            8, z, lambda k: bias.at[xl, 0, xh, k],
            lambda k: (bias.at[xl, 0, xh, k, pl.ds(0, 8)], bias.at[xl, 0, xh, k, pl.ds(8, 16)]), *z_args, 0,
        )
        b1 = Ring(
            4, x, lambda k: bias.at[lax.rem(k, 2), 1, k // 2, z],
            lambda k: (
                bias.at[lax.rem(k, 2), 1, k // 2, z, pl.ds(0, 8)],
                bias.at[lax.rem(k, 2), 1, k // 2, z, pl.ds(8, 16)],
            ), *x_args, 8,
        )
        a2 = Ring(
            4, x, lambda k: bias.at[lax.rem(k, 2), 0, k // 2],
            lambda k: (bias.at[lax.rem(k, 2), 0, k // 2, pl.ds(0, 4)], bias.at[lax.rem(k, 2), 0, k // 2, pl.ds(4, 4)]),
            *x_args, 16,
        )
        b2 = Ring(
            8, z, lambda k: bias.at[:, 1, :, k],
            lambda k: (bias.at[0, 1, :, k], bias.at[1, 1, :, k]), *z_args, 24,
        )

    a1.start()
    b1.start()

    def queries(u):
        if starting:
            spots = (4 * u + c, 4 * u + 2 + c)
        else:
            spots = (4 * u + 2 * c, 4 * u + 2 * c + 1)
        for r in range(ROWS):
            x_q = jnp.concatenate([rows[spots[0], r], rows[spots[1], r]], axis=0)
            qg = dot(x_q, w_qg, NN).astype(BF)
            big = dot(expand_ref[...], qg, NN)
            q_exp[u, r] = (big[:, :CH] * head_ref[...]).astype(BF)
            g_exp[u, r] = jax.nn.sigmoid(big[:, CH:]) * head_ref[...]

    queries(0)
    for step in range(1, 5):
        if 2 * step <= a1.n:
            a1.advance(step)
            if 2 * step == a1.n:
                a2.start()
        if 2 * step <= b1.n:
            b1.advance(step)
            if 2 * step == b1.n:
                b2.start()
    queries(1)
    a2.advance(1)
    b2.advance(1)
    queries(2)
    for step in range(2, 5):
        for ring in (a2, b2):
            if 2 * step <= ring.n:
                ring.advance(step)
        if step == 2:
            queries(3)

    if starting:
        line_at = TILE * (8 * xh + z)
        valid = [mask_smem[line_at + ROWS * me + r] for r in range(ROWS)]
    else:
        line_at = TILE * 2 * (4 * xl + y)
        valid = [mask_smem[line_at + TILE * (r // 3) + 3 * me + r % 3] for r in range(ROWS)]
    power = [v.astype(F32) * (INV_ROOT * LOG2E) for v in valid]
    bias_at = bias.reshape(SUPER, EXP, N)

    @pl.loop(0, SUPER)
    def _(u):
        for r in range(ROWS):
            for s in range(EXP // SUB):
                part = pl.ds(s * SUB, SUB)
                t = dot(q_exp[u, r, part], k_t[r], NN) + bias_at[u, part]
                top = jnp.max(t, axis=1, keepdims=True)
                e = jnp.exp2((t - top) * power[r]).astype(BF)
                o = dot(e, v_ext[r], NN)
                gat[u, r, part] = (g_exp[u, r, part] * (o[:, :CH] / o[:, CH:])).astype(BF)
            both = dot(collapse_ref[...], gat[u, r], NN).astype(BF)
            new = dot(both, w_out_ref[...], NN).astype(BF)
            upd[2 * u, r] = new[:TILE]
            upd[2 * u + 1, r] = new[TILE:]

    if starting:
        for d in range(1, n_peer):
            j = peer(d)
            copy = send(
                upd.at[j], ret.at[pl.ds(take * me, take)], r_send.at[d], r_recv.at[me], peer_place(j, c)
            )
            copy.start()
            sends.append(copy)
        ret[pl.ds(take * me, take)] = upd[me]
        for d in range(1, n_peer):
            j = peer(d)
            region = ret.at[pl.ds(take * j, take)]
            send(region, region, r_send.at[d], r_recv.at[j], sibling).wait_recv()
    else:
        mine = lax.rem(me // 2, 2) == c
        my_q = 2 * (me // 4) + lax.rem(me, 2)
        back = []
        for q in range(8):
            p = 4 * (q // 2) + 2 * c + q % 2
            for core in (0, 1):
                copy = send(
                    upd.at[q, pl.ds(3 * core, 3)],
                    ret.at[pl.ds(take * me, take)],
                    r_send.at[2 * q + core],
                    r_recv.at[me],
                    peer_place(p, core),
                )
                local = jnp.logical_and(p == me, c == core)

                @pl.when(jnp.logical_not(local))
                def _():
                    copy.start()

                back.append((local, copy))

        @pl.when(mine)
        def _():
            ret[pl.ds(take * me, take)] = upd[my_q, pl.ds(3 * c, 3)]

        for d in range(n_peer):
            j = peer(d)
            region = ret.at[pl.ds(take * j, take)]
            come = send(region, region, r_send.at[d], r_recv.at[j], sibling)
            if d == 0:

                @pl.when(jnp.logical_not(mine))
                def _():
                    come.wait_recv()

            else:
                come.wait_recv()
        for local, copy in back:

            @pl.when(jnp.logical_not(local))
            def _():
                copy.wait_send()

    out_ref[...] = ret[...]
    for copy in sends:
        copy.wait_send()

    @pl.when(source)
    def _():
        for d in range(1, n_first):
            first(d).wait_send()

    for ring in (a1, b1, a2, b2):
        ring.finish()


def expansion(starting):
    row = np.arange(EXP)
    if starting:
        blk, slot, r = row // 192, row % 192 // 24, row % 6
        pos = blk * TILE + 6 * slot + r
    else:
        slot, r6 = row // 24, row % 6
        pos = (r6 // 3) * TILE + 3 * slot + r6 % 3
    expand = (pos[:, None] == np.arange(POS)[None, :]).astype(np.float32)
    head = (row // 6 % HEADS)[:, None] == (np.arange(CH) // DIM)[None, :]
    return expand, head.astype(np.float32)


def node(starting, tile, mask, w_proj, w_bias, w_out):
    expand, head = expansion(starting)
    vmem = pl.BlockSpec(memory_space=pltpu.VMEM)
    smem = pl.BlockSpec(memory_space=pltpu.SMEM)
    dma = pltpu.SemaphoreType.DMA
    if starting:
        bias_shape = (2, 4, 2, 4, 24, N)
    else:
        bias_shape = (2, 2, 2, 8, 24, N)
    return pl.pallas_call(
        functools.partial(node_kernel, starting),
        out_shape=jax.ShapeDtypeStruct((TILE, TILE, CH), BF),
        in_specs=[vmem, smem] + [vmem] * 7,
        out_specs=vmem,
        scratch_shapes=[
            pltpu.VMEM((TILE, TILE, CH), BF),
            pltpu.VMEM((16, ROWS, TILE, CH), BF),
            pltpu.VMEM(bias_shape, F32),
            pltpu.VMEM((ROWS, CH, N), BF),
            pltpu.VMEM((ROWS, N, 2 * CH), BF),
            pltpu.VMEM((SUPER, ROWS, EXP, CH), BF),
            pltpu.VMEM((SUPER, ROWS, EXP, CH), F32),
            pltpu.VMEM((SUPER, ROWS, EXP, CH), BF),
            pltpu.VMEM((8, ROWS, TILE, CH), BF),
            pltpu.VMEM((TILE, TILE, CH), BF),
            dma((16,)),
            dma((16,)),
            dma((16,)),
            dma((16,)),
            dma((8,)),
            dma((4,)),
            dma((32,)),
            dma((32,)),
            dma((16,)),
            dma((16,)),
        ],
        compiler_params=pltpu.CompilerParams(
            collective_id=0 if starting else 1, has_side_effects=True, vmem_limit_bytes=56 * 1024 * 1024
        ),
        name="start_node" if starting else "end_node",
    )(
        tile,
        mask,
        mask.reshape(1, N),
        w_proj,
        w_bias,
        w_out,
        jnp.asarray(expand, BF),
        jnp.asarray(expand.T, BF),
        jnp.asarray(head, F32),
    )


def on_device(pair_act, mask, w_proj_start, w_bias_start, w_out_start, w_proj_end, w_bias_end, w_out_end):
    update_start = node(True, pair_act, mask, w_proj_start, w_bias_start, w_out_start)
    updated = pair_act.astype(F32) + update_start.astype(F32)
    flipped = jnp.swapaxes(layer_norm(updated), 0, 1)
    update_end = node(False, flipped, mask, w_proj_end, w_bias_end, w_out_end)
    return update_start, jnp.swapaxes(update_end, 0, 1)


def solution(mesh):
    split = Mesh(mesh.devices.reshape(SIZES), AXES)
    placed = (P(WIDE, NARROW, None),) + (P(),) * 7
    return jax.shard_map(
        on_device,
        mesh=split,
        in_specs=placed,
        out_specs=(P(WIDE, NARROW, None), P(WIDE, NARROW, None)),
        check_vma=False,
    )
```

```python
import functools
import math

import jax
import jax.numpy as jnp
import numpy as np
from jax import lax
from jax.experimental import pallas as pl
from jax.experimental.pallas import tpu as pltpu
from jax.sharding import Mesh
from jax.sharding import PartitionSpec as P

AXES = ("xh", "z", "xl", "y", "c")
SIZES = (2, 8, 2, 4, 2)
NARROW = ("xl", "y", "c")
WIDE = ("xh", "z")

HEADS = 4
DIM = 32
CH = HEADS * DIM
TILE = 48
N = 768
ROWS = 6
SUPER = 4
POS = 2 * TILE
EXP = POS * HEADS
SUB = 192
NORM_EPS = 1e-05
MASKED = -1000000000.0
INV_ROOT = DIM ** (-0.5)
ROOT = math.sqrt(DIM)
LOG2E = math.log2(math.e)
BF = jnp.bfloat16
F32 = jnp.float32


def layer_norm(features):
    average = jnp.mean(features, axis=-1, keepdims=True)
    centred = features - average
    spread = jnp.mean(centred * centred, axis=-1, keepdims=True)
    return (centred * lax.rsqrt(spread + NORM_EPS)).astype(BF)


def here():
    return {a: lax.axis_index(a) for a in AXES}


def place(at, **kw):
    return tuple(kw.get(a, at[a]) for a in AXES)


def dot(a, b, dims):
    return lax.dot_general(a, b, (dims, ((), ())), preferred_element_type=F32)


NN = ((1,), (0,))
NT = ((1,), (1,))


def send(src, dst, ssem, rsem, device):
    return pltpu.make_async_remote_copy(
        src_ref=src,
        dst_ref=dst,
        send_sem=ssem,
        recv_sem=rsem,
        device_id=device,
        device_id_type=pl.DeviceIdType.MESH,
    )


class Ring:
    def __init__(self, n, idx, whole, halves, plus, minus, ssem, rsem, base, has=None):
        self.n, self.idx, self.has = n, idx, has
        self.whole, self.halves = whole, halves
        self.plus, self.minus = plus, minus
        self.ssem, self.rsem, self.base = ssem, rsem, base

    def block(self, offset):
        return lax.rem(self.idx + offset + self.n, self.n)

    def copy(self, step, way, block):
        region = self.halves(block)[way] if 2 * step == self.n else self.whole(block)
        at = self.base + 2 * (step - 1) + way
        return send(region, region, self.ssem.at[at], self.rsem.at[at], self.minus if way else self.plus)

    def where(self, block, do):
        if self.has is None:
            do()
        else:
            pl.when(self.has(block))(do)

    def start(self):
        for way in (0, 1):
            self.where(self.idx, lambda: self.copy(1, way, self.idx).start())

    def advance(self, step):
        for way in (0, 1):
            came = self.block(step if way else -step)

            def do():
                self.copy(step, way, came).wait_recv()
                if 2 * step < self.n:
                    self.copy(step + 1, way, came).start()

            self.where(came, do)

    def finish(self):
        for step in range(1, self.n // 2 + 1):
            for way in (0, 1):
                block = self.block(step - 1 if way else 1 - step)
                self.where(block, lambda: self.copy(step, way, block).wait_send())


def picker(offset, transposed):
    shape = (CH, 4 * CH) if transposed else (4 * CH, CH)
    d = lax.broadcasted_iota(jnp.int32, shape, 0 if transposed else 1)
    x = lax.broadcasted_iota(jnp.int32, shape, 1 if transposed else 0)
    return jnp.where(x == (d >> 5) * CH + offset * DIM + (d & 31), 1.0, 0.0).astype(BF)


def node_kernel(
    starting,
    tile_ref,
    mask_smem,
    key_ok_ref,
    w_proj_ref,
    w_bias_ref,
    w_out_ref,
    expand_ref,
    collapse_ref,
    head_ref,
    out_ref,
    nt,
    rows,
    bias,
    k_t,
    v_ext,
    q_exp,
    g_exp,
    gat,
    upd,
    ret,
    a_send,
    a_recv,
    f_send,
    f_recv,
    p_send,
    p_recv,
    g_send,
    g_recv,
    r_send,
    r_recv,
):
    at = here()
    xh, z, xl, y, c = (at[a] for a in AXES)
    x = 2 * xh + xl
    other = 1 - c
    if starting:
        n_peer, take = 8, 6
        me = xl * 4 + y
        peer_place = lambda j, core: place(at, xl=j // 4, y=lax.rem(j, 4), c=core)
        slot = lambda j, core: (2 * j + core, slice(None))
    else:
        n_peer, take = 16, 3
        me = xh * 8 + z
        peer_place = lambda j, core: place(at, xh=j // 8, z=lax.rem(j, 8), c=core)
        slot = lambda j, core: (j, pl.ds(3 * core, 3))

    def peer(d):
        return lax.rem(me + d, n_peer)

    def x_place(step):
        to = lax.rem(x + step + 4, 4)
        return place(at, xh=to // 2, xl=lax.rem(to, 2))

    y_place = lambda step: place(at, y=lax.rem(y + step + 4, 4))
    z_place = lambda step: place(at, z=lax.rem(z + step + 8, 8))
    sibling = place(at, c=other)

    partners = [peer_place(peer(d), c) for d in range(1, n_peer)]
    partners.append(sibling)
    if starting:
        partners += [z_place(d) for d in range(1, 8)]
        far = lax.rem(x + jnp.where(xl == 0, 3, 1), 4)
        partners.append(place(at, xh=far // 2, xl=lax.rem(far, 2)))
    else:
        partners += [peer_place(peer(d), other) for d in range(1, n_peer)]
        partners += [y_place(d) for d in range(1, 4)]
        partners += [x_place(1), x_place(-1)]
    barrier = pltpu.get_barrier_semaphore()
    for partner in partners:
        pl.semaphore_signal(barrier, inc=1, device_id=partner, device_id_type=pl.DeviceIdType.MESH)

    if starting:
        nt[...] = layer_norm(tile_ref[...].astype(F32))
        out_tile = nt
    else:
        out_tile = tile_ref
    own = out_tile[pl.ds(take * me, take)]
    rows[slot(me, c)] = own
    pl.semaphore_wait(barrier, len(partners))

    sends = []
    for d in range(1, n_peer):
        j = peer(d)
        copy = send(
            out_tile.at[pl.ds(take * j, take)],
            rows.at[slot(me, c)],
            a_send.at[d],
            a_recv.at[me],
            peer_place(j, c),
        )
        copy.start()
        sends.append(copy)

    def forward(d):
        j = peer(d)
        region = rows.at[slot(j, c)]
        copy = send(region, region, f_send.at[d], f_recv.at[j], sibling)
        copy.start()
        sends.append(copy)

    forward(0)

    w_all = w_proj_ref[...]
    w_kt = dot(picker(1, True), w_all, NT).astype(BF)
    w_v = dot(w_all, picker(2, False), NN).astype(BF)
    w_qg = jnp.concatenate([dot(w_all, picker(0, False), NN), dot(w_all, picker(3, False), NN)], axis=1).astype(BF)
    s_row = lax.broadcasted_iota(jnp.int32, (24, HEADS), 0)
    s_head = lax.broadcasted_iota(jnp.int32, (24, HEADS), 1)
    w_bias = w_bias_ref[...]
    w_rows = [
        dot(jnp.where(s_row == s_head * ROWS + r, 1.0, 0.0).astype(BF), w_bias, NT).astype(BF) for r in range(ROWS)
    ]

    for d in range(1, n_peer):
        j = peer(d)
        region = rows.at[slot(j, c)]
        send(region, region, a_send.at[d], a_recv.at[j], sibling).wait_recv()
        forward(d)
    for d in range(n_peer):
        j = peer(d)
        region = rows.at[slot(j, other)]
        send(region, region, f_send.at[d], f_recv.at[j], sibling).wait_recv()

    piece = jnp.zeros((24, N), F32)
    for r in range(ROWS):
        piece += dot(w_rows[r], rows[:, r].reshape(N, CH), NT)
    piece = jnp.where(key_ok_ref[...] > 0, piece * ROOT, MASKED)
    y2 = y // 2
    if starting:
        source = lax.rem(z, 2) == c
        own_piece = bias.at[xh, z // 2, xl, y]
        part = lambda k: bias.at[xh, k // 2, xl, y]
        comes = lambda k: jnp.logical_and(lax.rem(k, 2) == c, k != z)
    else:
        source = lax.rem(y, 2) == c
        own_piece = bias.at[xl, y2, xh, z]
        part = lambda k: bias.at[xl, y2, xh, k]
        comes = lambda k: jnp.logical_and(source, k != z)

    def first(d):
        return send(own_piece, own_piece, p_send.at[d], p_recv.at[z], z_place(d))

    @pl.when(source)
    def _():
        own_piece[...] = piece
        for d in range(1, 8):
            first(d).start()

    for r in range(ROWS):
        x_r = rows[:, r].reshape(N, CH)
        k_t[r] = dot(w_kt, x_r, NT).astype(BF)
        v_ext[r, :, :CH] = dot(x_r, w_v, NN).astype(BF)
        v_ext[r, :, CH:] = jnp.ones((N, CH), BF)

    def queries(u, r):
        if starting:
            spots = (4 * u + c, 4 * u + 2 + c)
        else:
            spots = (4 * u + 2 * c, 4 * u + 2 * c + 1)
        x_q = jnp.concatenate([rows[spots[0], r], rows[spots[1], r]], axis=0)
        qg = dot(x_q, w_qg, NN).astype(BF)
        big = dot(expand_ref[...], qg, NN)
        q = (big[:, :CH] * head_ref[...]).reshape(*lead, 24, CH)
        g = (jax.nn.sigmoid(big[:, CH:]) * head_ref[...]).reshape(*lead, 24, CH)
        q_exp[(r, *in_super(u))] = q
        g_exp[(r, *in_super(u))] = g

    if starting:
        lead = (2, 2, 4)
        in_super = lambda u: (u // 2, pl.ds(2 * (u % 2), 2))
    else:
        lead = (2, 8)
        in_super = lambda u: (u // 2, u % 2)

    for r in range(ROWS):
        queries(0, r)
        queries(1, r)

    for k in range(8):

        @pl.when(comes(k))
        def _():
            send(part(k), part(k), p_send.at[0], p_recv.at[k], sibling).wait_recv()

    x_args = (x_place(1), x_place(-1), g_send, g_recv)
    y_args = (y_place(1), y_place(-1), g_send, g_recv)
    if starting:
        a1 = Ring(
            4, y, lambda k: bias.at[xh, pl.ds(0, 2), xl, k],
            lambda k: (bias.at[xh, 0, xl, k], bias.at[xh, 1, xl, k]), *y_args, 0,
        )
        b1 = Ring(
            4, x, lambda k: bias.at[k // 2, pl.ds(2, 2), lax.rem(k, 2), y],
            lambda k: (bias.at[k // 2, 2, lax.rem(k, 2), y], bias.at[k // 2, 3, lax.rem(k, 2), y]), *x_args, 4,
        )
        a2 = Ring(
            4, x, lambda k: bias.at[k // 2, pl.ds(0, 2), lax.rem(k, 2)],
            lambda k: (bias.at[k // 2, 0, lax.rem(k, 2)], bias.at[k // 2, 1, lax.rem(k, 2)]), *x_args, 8,
        )
        b2 = Ring(
            4, y, lambda k: bias.at[:, pl.ds(2, 2), :, k],
            lambda k: (bias.at[:, 2, :, k], bias.at[:, 3, :, k]), *y_args, 12,
        )
    else:
        has = lambda k: lax.rem(k, 2) == c
        here_only = lambda k: source
        a1 = Ring(
            4, y, lambda k: bias.at[xl, k // 2, xh, pl.ds(0, 4)],
            lambda k: (bias.at[xl, k // 2, xh, pl.ds(0, 2)], bias.at[xl, k // 2, xh, pl.ds(2, 2)]), *y_args, 0, has,
        )
        b1 = Ring(
            4, x, lambda k: bias.at[lax.rem(k, 2), y2, k // 2, pl.ds(4, 4)],
            lambda k: (
                bias.at[lax.rem(k, 2), y2, k // 2, pl.ds(4, 2)],
                bias.at[lax.rem(k, 2), y2, k // 2, pl.ds(6, 2)],
            ), *x_args, 4, here_only,
        )
        a2 = Ring(
            4, x, lambda k: bias.at[lax.rem(k, 2), :, k // 2, pl.ds(0, 4)],
            lambda k: (
                bias.at[lax.rem(k, 2), 0, k // 2, pl.ds(0, 4)],
                bias.at[lax.rem(k, 2), 1, k // 2, pl.ds(0, 4)],
            ), *x_args, 8,
        )
        b2 = Ring(
            4, y, lambda k: bias.at[:, k // 2, :, pl.ds(4, 4)],
            lambda k: (bias.at[0, k // 2, :, pl.ds(4, 4)], bias.at[1, k // 2, :, pl.ds(4, 4)]), *y_args, 12, has,
        )

    a1.start()
    b1.start()
    for r in range(ROWS):
        queries(2, r)
    a1.advance(1)
    b1.advance(1)
    for r in range(ROWS):
        queries(3, r)
    a1.advance(2)
    b1.advance(2)
    a2.start()
    b2.start()

    if starting:
        line_at = TILE * (8 * xh + z)
        valid = [mask_smem[line_at + ROWS * me + r] for r in range(ROWS)]
    else:
        line_at = TILE * 2 * (4 * xl + y)
        valid = [mask_smem[line_at + TILE * (r // 3) + 3 * me + r % 3] for r in range(ROWS)]
    power = [v.astype(F32) * (INV_ROOT * LOG2E) for v in valid]

    def attend(at):
        pairs = bias[at].reshape(SUB, N)
        for r in range(ROWS):
            t = dot(q_exp[(r, *at)].reshape(SUB, CH).astype(BF), k_t[r], NN) + pairs
            top = jnp.max(t, axis=1, keepdims=True)
            e = jnp.exp2((t - top) * power[r]).astype(BF)
            o = dot(e, v_ext[r], NN)
            gated = g_exp[(r, *at)].reshape(SUB, CH) * (o[:, :CH] / o[:, CH:])
            gat[(r, *at)] = gated.reshape(*q_exp[(r, *at)].shape)

    @pl.loop(0, 4)
    def _(t):
        step = jnp.where(t == 3, 2, jnp.where(t == 2, 3, t))

        @pl.when(t == 1)
        def _():
            a2.advance(1)
            if starting:
                b2.advance(1)

        @pl.when(t == 2)
        def _():
            if not starting:
                b2.advance(2)

        @pl.when(t == 3)
        def _():
            a2.advance(2)
            if starting:
                b2.advance(2)

        xc = lax.rem(x + step, 4)
        if starting:
            attend((xc // 2, pl.ds(0, 2), lax.rem(xc, 2)))
            attend((slice(None), pl.ds(2, 2), slice(None), lax.rem(y + step, 4)))
        else:
            attend((lax.rem(xc, 2), slice(None), xc // 2, pl.ds(0, 4)))

            @pl.when(t == 0)
            def _():
                b2.advance(1)

            y_c = jnp.where(t < 2, y2, 1 - y2)
            attend((lax.rem(t, 2), y_c, slice(None), pl.ds(4, 4)))

    for u in range(SUPER):
        for r in range(ROWS):
            wide = gat[(r, *in_super(u))].reshape(EXP, CH).astype(BF)
            both = dot(collapse_ref[...], wide, NN).astype(BF)
            new = dot(both, w_out_ref[...], NN).astype(BF)
            upd[2 * u, r] = new[:TILE]
            upd[2 * u + 1, r] = new[TILE:]

    if starting:
        for d in range(1, n_peer):
            j = peer(d)
            copy = send(
                upd.at[j], ret.at[pl.ds(take * me, take)], r_send.at[d], r_recv.at[me], peer_place(j, c)
            )
            copy.start()
            sends.append(copy)
        ret[pl.ds(take * me, take)] = upd[me]
        for d in range(1, n_peer):
            j = peer(d)
            region = ret.at[pl.ds(take * j, take)]
            send(region, region, r_send.at[d], r_recv.at[j], sibling).wait_recv()
    else:
        mine = lax.rem(me // 2, 2) == c
        my_q = 2 * (me // 4) + lax.rem(me, 2)
        back = []
        for q in range(8):
            p = 4 * (q // 2) + 2 * c + q % 2
            for core in (0, 1):
                copy = send(
                    upd.at[q, pl.ds(3 * core, 3)],
                    ret.at[pl.ds(take * me, take)],
                    r_send.at[2 * q + core],
                    r_recv.at[me],
                    peer_place(p, core),
                )
                local = jnp.logical_and(p == me, c == core)

                @pl.when(jnp.logical_not(local))
                def _():
                    copy.start()

                back.append((local, copy))

        @pl.when(mine)
        def _():
            ret[pl.ds(take * me, take)] = upd[my_q, pl.ds(3 * c, 3)]

        for d in range(n_peer):
            j = peer(d)
            region = ret.at[pl.ds(take * j, take)]
            come = send(region, region, r_send.at[d], r_recv.at[j], sibling)
            if d == 0:

                @pl.when(jnp.logical_not(mine))
                def _():
                    come.wait_recv()

            else:
                come.wait_recv()
        for local, copy in back:

            @pl.when(jnp.logical_not(local))
            def _():
                copy.wait_send()

    out_ref[...] = ret[...]
    for copy in sends:
        copy.wait_send()

    @pl.when(source)
    def _():
        for d in range(1, 8):
            first(d).wait_send()

    for ring in (a1, b1, a2, b2):
        ring.finish()


def expansion(starting):
    row = np.arange(EXP)
    if starting:
        blk, slot, r = row // 192, row % 192 // 24, row % 6
        pos = blk * TILE + 6 * slot + r
    else:
        slot, r6 = row // 24, row % 6
        pos = (r6 // 3) * TILE + 3 * slot + r6 % 3
    expand = (pos[:, None] == np.arange(POS)[None, :]).astype(np.float32)
    head = (row // 6 % HEADS)[:, None] == (np.arange(CH) // DIM)[None, :]
    return expand, head.astype(np.float32)


def node(starting, tile, mask, w_proj, w_bias, w_out):
    expand, head = expansion(starting)
    vmem = pl.BlockSpec(memory_space=pltpu.VMEM)
    smem = pl.BlockSpec(memory_space=pltpu.SMEM)
    dma = pltpu.SemaphoreType.DMA
    if starting:
        bias_shape = (2, 4, 2, 4, 24, N)
    else:
        bias_shape = (2, 2, 2, 8, 24, N)
    return pl.pallas_call(
        functools.partial(node_kernel, starting),
        out_shape=jax.ShapeDtypeStruct((TILE, TILE, CH), BF),
        in_specs=[vmem, smem] + [vmem] * 7,
        out_specs=vmem,
        scratch_shapes=[
            pltpu.VMEM((TILE, TILE, CH), BF),
            pltpu.VMEM((16, ROWS, TILE, CH), BF),
            pltpu.VMEM(bias_shape, F32),
            pltpu.VMEM((ROWS, CH, N), BF),
            pltpu.VMEM((ROWS, N, 2 * CH), BF),
            pltpu.VMEM((ROWS, *bias_shape[:-1], CH), F32),
            pltpu.VMEM((ROWS, *bias_shape[:-1], CH), F32),
            pltpu.VMEM((ROWS, *bias_shape[:-1], CH), F32),
            pltpu.VMEM((8, ROWS, TILE, CH), BF),
            pltpu.VMEM((TILE, TILE, CH), BF),
            dma((16,)),
            dma((16,)),
            dma((16,)),
            dma((16,)),
            dma((8,)),
            dma((8,)),
            dma((16,)),
            dma((16,)),
            dma((16,)),
            dma((16,)),
        ],
        compiler_params=pltpu.CompilerParams(
            collective_id=0 if starting else 1, has_side_effects=True, vmem_limit_bytes=56 * 1024 * 1024
        ),
        name="start_node" if starting else "end_node",
    )(
        tile,
        mask,
        mask.reshape(1, N),
        w_proj,
        w_bias,
        w_out,
        jnp.asarray(expand, BF),
        jnp.asarray(expand.T, BF),
        jnp.asarray(head, F32),
    )


def on_device(pair_act, mask, w_proj_start, w_bias_start, w_out_start, w_proj_end, w_bias_end, w_out_end):
    update_start = node(True, pair_act, mask, w_proj_start, w_bias_start, w_out_start)
    updated = pair_act.astype(F32) + update_start.astype(F32)
    flipped = jnp.swapaxes(layer_norm(updated), 0, 1)
    update_end = node(False, flipped, mask, w_proj_end, w_bias_end, w_out_end)
    return update_start, jnp.swapaxes(update_end, 0, 1)


def solution(mesh):
    split = Mesh(mesh.devices.reshape(SIZES), AXES)
    placed = (P(WIDE, NARROW, None),) + (P(),) * 7
    return jax.shard_map(
        on_device,
        mesh=split,
        in_specs=placed,
        out_specs=(P(WIDE, NARROW, None), P(WIDE, NARROW, None)),
        check_vma=False,
    )
```

```python
import functools
import math

import jax
import jax.numpy as jnp
import numpy as np
from jax import lax
from jax.experimental import pallas as pl
from jax.experimental.pallas import tpu as pltpu
from jax.sharding import Mesh
from jax.sharding import PartitionSpec as P

AXES = ("xh", "z", "xl", "y", "c")
SIZES = (2, 8, 2, 4, 2)
NARROW = ("xl", "y", "c")
WIDE = ("xh", "z")

HEADS = 4
DIM = 32
CH = HEADS * DIM
TILE = 48
N = 768
ROWS = 6
SUPER = 4
POS = 2 * TILE
EXP = POS * HEADS
SUB = 192
NORM_EPS = 1e-05
MASKED = -1000000000.0
INV_ROOT = DIM ** (-0.5)
ROOT = math.sqrt(DIM)
LOG2E = math.log2(math.e)
BF = jnp.bfloat16
F32 = jnp.float32


def layer_norm(features):
    average = jnp.mean(features, axis=-1, keepdims=True)
    centred = features - average
    spread = jnp.mean(centred * centred, axis=-1, keepdims=True)
    return (centred * lax.rsqrt(spread + NORM_EPS)).astype(BF)


def here():
    return {a: lax.axis_index(a) for a in AXES}


def place(at, **kw):
    return tuple(kw.get(a, at[a]) for a in AXES)


def dot(a, b, dims):
    return lax.dot_general(a, b, (dims, ((), ())), preferred_element_type=F32)


NN = ((1,), (0,))
NT = ((1,), (1,))


def send(src, dst, ssem, rsem, device):
    return pltpu.make_async_remote_copy(
        src_ref=src,
        dst_ref=dst,
        send_sem=ssem,
        recv_sem=rsem,
        device_id=device,
        device_id_type=pl.DeviceIdType.MESH,
    )


class Ring:
    def __init__(self, n, idx, whole, halves, plus, minus, ssem, rsem, base, has=None):
        self.n, self.idx, self.has = n, idx, has
        self.whole, self.halves = whole, halves
        self.plus, self.minus = plus, minus
        self.ssem, self.rsem, self.base = ssem, rsem, base

    def block(self, offset):
        return lax.rem(self.idx + offset + self.n, self.n)

    def copy(self, step, way, block):
        region = self.halves(block)[way] if 2 * step == self.n else self.whole(block)
        at = self.base + 2 * (step - 1) + way
        return send(region, region, self.ssem.at[at], self.rsem.at[at], self.minus if way else self.plus)

    def where(self, block, do):
        if self.has is None:
            do()
        else:
            pl.when(self.has(block))(do)

    def start(self):
        for way in (0, 1):
            self.where(self.idx, lambda: self.copy(1, way, self.idx).start())

    def advance(self, step):
        for way in (0, 1):
            came = self.block(step if way else -step)

            def do():
                self.copy(step, way, came).wait_recv()
                if 2 * step < self.n:
                    self.copy(step + 1, way, came).start()

            self.where(came, do)

    def finish(self):
        for step in range(1, self.n // 2 + 1):
            for way in (0, 1):
                block = self.block(step - 1 if way else 1 - step)
                self.where(block, lambda: self.copy(step, way, block).wait_send())


def picker(offset, transposed):
    shape = (CH, 4 * CH) if transposed else (4 * CH, CH)
    d = lax.broadcasted_iota(jnp.int32, shape, 0 if transposed else 1)
    x = lax.broadcasted_iota(jnp.int32, shape, 1 if transposed else 0)
    return jnp.where(x == (d >> 5) * CH + offset * DIM + (d & 31), 1.0, 0.0).astype(BF)


def run(starting, b, barrier_done, out_tile, rows, bias, ret, sems):
    mask_smem, key_ok, w_proj_ref, w_bias_ref, w_out_ref, expand_ref, collapse_ref, head_ref = b.given[starting]
    k_t, v_ext, upd = b.k_t, b.v_ext, b.upd
    q_exp, g_exp, gat = (ref.reshape(ROWS, *bias.shape[:-1], CH) for ref in (b.q_exp, b.g_exp, b.gat))
    a_send, a_recv, f_send, f_recv, p_send, p_recv, g_send, g_recv, r_send, r_recv = sems
    at = here()
    xh, z, xl, y, c = (at[a] for a in AXES)
    x = 2 * xh + xl
    other = 1 - c
    if starting:
        n_peer, take = 8, 6
        me = xl * 4 + y
        peer_place = lambda j, core: place(at, xl=j // 4, y=lax.rem(j, 4), c=core)
        slot = lambda j, core: (2 * j + core, slice(None))
    else:
        n_peer, take = 16, 3
        me = xh * 8 + z
        peer_place = lambda j, core: place(at, xh=j // 8, z=lax.rem(j, 8), c=core)
        slot = lambda j, core: (j, pl.ds(3 * core, 3))

    def peer(d):
        return lax.rem(me + d, n_peer)

    def x_place(step):
        to = lax.rem(x + step + 4, 4)
        return place(at, xh=to // 2, xl=lax.rem(to, 2))

    y_place = lambda step: place(at, y=lax.rem(y + step + 4, 4))
    z_place = lambda step: place(at, z=lax.rem(z + step + 8, 8))
    sibling = place(at, c=other)

    own = out_tile[pl.ds(take * me, take)]
    rows[slot(me, c)] = own
    barrier_done()

    sends = []
    for d in range(1, n_peer):
        j = peer(d)
        copy = send(
            out_tile.at[pl.ds(take * j, take)],
            rows.at[slot(me, c)],
            a_send.at[d],
            a_recv.at[me],
            peer_place(j, c),
        )
        copy.start()
        sends.append(copy)

    def forward(d):
        j = peer(d)
        region = rows.at[slot(j, c)]
        copy = send(region, region, f_send.at[d], f_recv.at[j], sibling)
        copy.start()
        sends.append(copy)

    forward(0)

    w_all = w_proj_ref[...]
    w_kt = dot(picker(1, True), w_all, NT).astype(BF)
    w_v = dot(w_all, picker(2, False), NN).astype(BF)
    w_qg = jnp.concatenate([dot(w_all, picker(0, False), NN), dot(w_all, picker(3, False), NN)], axis=1).astype(BF)
    s_row = lax.broadcasted_iota(jnp.int32, (24, HEADS), 0)
    s_head = lax.broadcasted_iota(jnp.int32, (24, HEADS), 1)
    w_bias = w_bias_ref[...]
    w_rows = [
        dot(jnp.where(s_row == s_head * ROWS + r, 1.0, 0.0).astype(BF), w_bias, NN).astype(BF) for r in range(ROWS)
    ]

    for d in range(1, n_peer):
        j = peer(d)
        region = rows.at[slot(j, c)]
        send(region, region, a_send.at[d], a_recv.at[j], sibling).wait_recv()
        forward(d)
    for d in range(n_peer):
        j = peer(d)
        region = rows.at[slot(j, other)]
        send(region, region, f_send.at[d], f_recv.at[j], sibling).wait_recv()

    piece = jnp.zeros((24, N), F32)
    for r in range(ROWS):
        piece += dot(w_rows[r], rows[:, r].reshape(N, CH), NT)
    piece = jnp.where(key_ok > 0, piece * ROOT, MASKED)
    y2 = y // 2
    if starting:
        source = lax.rem(z, 2) == c
        own_piece = bias.at[xh, z // 2, xl, y]
        part = lambda k: bias.at[xh, k // 2, xl, y]
        comes = lambda k: jnp.logical_and(lax.rem(k, 2) == c, k != z)
    else:
        source = lax.rem(y, 2) == c
        own_piece = bias.at[xl, y2, xh, z]
        part = lambda k: bias.at[xl, y2, xh, k]
        comes = lambda k: jnp.logical_and(source, k != z)

    def first(d):
        return send(own_piece, own_piece, p_send.at[d], p_recv.at[z], z_place(d))

    @pl.when(source)
    def _():
        own_piece[...] = piece
        for d in range(1, 8):
            first(d).start()

    for r in range(ROWS):
        x_r = rows[:, r].reshape(N, CH)
        k_t[r] = dot(w_kt, x_r, NT).astype(BF)
        v_ext[r, :, :CH] = dot(x_r, w_v, NN).astype(BF)
        v_ext[r, :, CH:] = jnp.ones((N, CH), BF)

    def queries(u, r):
        if starting:
            spots = (4 * u + c, 4 * u + 2 + c)
        else:
            spots = (4 * u + 2 * c, 4 * u + 2 * c + 1)
        x_q = jnp.concatenate([rows[spots[0], r], rows[spots[1], r]], axis=0)
        qg = dot(x_q, w_qg, NN).astype(BF)
        big = dot(expand_ref[...], qg, NN)
        q = (big[:, :CH] * head_ref[...]).reshape(*lead, 24, CH)
        g = (jax.nn.sigmoid(big[:, CH:]) * head_ref[...]).reshape(*lead, 24, CH)
        q_exp[(r, *in_super(u))] = q
        g_exp[(r, *in_super(u))] = g

    if starting:
        lead = (2, 2, 4)
        in_super = lambda u: (u // 2, pl.ds(2 * (u % 2), 2))
    else:
        lead = (2, 8)
        in_super = lambda u: (u // 2, u % 2)

    for r in range(ROWS):
        queries(0, r)
        queries(1, r)

    for k in range(8):

        @pl.when(comes(k))
        def _():
            send(part(k), part(k), p_send.at[0], p_recv.at[k], sibling).wait_recv()

    x_args = (x_place(1), x_place(-1), g_send, g_recv)
    y_args = (y_place(1), y_place(-1), g_send, g_recv)
    if starting:
        a1 = Ring(
            4, y, lambda k: bias.at[xh, pl.ds(0, 2), xl, k],
            lambda k: (bias.at[xh, 0, xl, k], bias.at[xh, 1, xl, k]), *y_args, 0,
        )
        b1 = Ring(
            4, x, lambda k: bias.at[k // 2, pl.ds(2, 2), lax.rem(k, 2), y],
            lambda k: (bias.at[k // 2, 2, lax.rem(k, 2), y], bias.at[k // 2, 3, lax.rem(k, 2), y]), *x_args, 4,
        )
        a2 = Ring(
            4, x, lambda k: bias.at[k // 2, pl.ds(0, 2), lax.rem(k, 2)],
            lambda k: (bias.at[k // 2, 0, lax.rem(k, 2)], bias.at[k // 2, 1, lax.rem(k, 2)]), *x_args, 8,
        )
        b2 = Ring(
            4, y, lambda k: bias.at[:, pl.ds(2, 2), :, k],
            lambda k: (bias.at[:, 2, :, k], bias.at[:, 3, :, k]), *y_args, 12,
        )
    else:
        has = lambda k: lax.rem(k, 2) == c
        here_only = lambda k: source
        a1 = Ring(
            4, y, lambda k: bias.at[xl, k // 2, xh, pl.ds(0, 4)],
            lambda k: (bias.at[xl, k // 2, xh, pl.ds(0, 2)], bias.at[xl, k // 2, xh, pl.ds(2, 2)]), *y_args, 0, has,
        )
        b1 = Ring(
            4, x, lambda k: bias.at[lax.rem(k, 2), y2, k // 2, pl.ds(4, 4)],
            lambda k: (
                bias.at[lax.rem(k, 2), y2, k // 2, pl.ds(4, 2)],
                bias.at[lax.rem(k, 2), y2, k // 2, pl.ds(6, 2)],
            ), *x_args, 4, here_only,
        )
        a2 = Ring(
            4, x, lambda k: bias.at[lax.rem(k, 2), :, k // 2, pl.ds(0, 4)],
            lambda k: (
                bias.at[lax.rem(k, 2), 0, k // 2, pl.ds(0, 4)],
                bias.at[lax.rem(k, 2), 1, k // 2, pl.ds(0, 4)],
            ), *x_args, 8,
        )
        b2 = Ring(
            4, y, lambda k: bias.at[:, k // 2, :, pl.ds(4, 4)],
            lambda k: (bias.at[0, k // 2, :, pl.ds(4, 4)], bias.at[1, k // 2, :, pl.ds(4, 4)]), *y_args, 12, has,
        )

    a1.start()
    b1.start()
    for r in range(ROWS):
        queries(2, r)
    a1.advance(1)
    b1.advance(1)
    for r in range(ROWS):
        queries(3, r)
    a1.advance(2)
    b1.advance(2)
    a2.start()
    b2.start()

    if starting:
        line_at = TILE * (8 * xh + z)
        valid = [mask_smem[line_at + ROWS * me + r] for r in range(ROWS)]
    else:
        line_at = TILE * 2 * (4 * xl + y)
        valid = [mask_smem[line_at + TILE * (r // 3) + 3 * me + r % 3] for r in range(ROWS)]
    power = [v.astype(F32) * (INV_ROOT * LOG2E) for v in valid]

    def attend(at):
        pairs = bias[at].reshape(SUB, N)
        for r in range(ROWS):
            t = dot(q_exp[(r, *at)].reshape(SUB, CH).astype(BF), k_t[r], NN) + pairs
            top = jnp.max(t, axis=1, keepdims=True)
            e = jnp.exp2((t - top) * power[r]).astype(BF)
            o = dot(e, v_ext[r], NN)
            gated = g_exp[(r, *at)].reshape(SUB, CH) * (o[:, :CH] / o[:, CH:])
            gat[(r, *at)] = gated.reshape(*q_exp[(r, *at)].shape)

    @pl.loop(0, 4)
    def _(t):
        step = jnp.where(t == 3, 2, jnp.where(t == 2, 3, t))

        @pl.when(t == 1)
        def _():
            a2.advance(1)
            if starting:
                b2.advance(1)

        @pl.when(t == 2)
        def _():
            if not starting:
                b2.advance(2)

        @pl.when(t == 3)
        def _():
            a2.advance(2)
            if starting:
                b2.advance(2)

        xc = lax.rem(x + step, 4)
        if starting:
            attend((xc // 2, pl.ds(0, 2), lax.rem(xc, 2)))
            attend((slice(None), pl.ds(2, 2), slice(None), lax.rem(y + step, 4)))
        else:
            attend((lax.rem(xc, 2), slice(None), xc // 2, pl.ds(0, 4)))

            @pl.when(t == 0)
            def _():
                b2.advance(1)

            y_c = jnp.where(t < 2, y2, 1 - y2)
            attend((lax.rem(t, 2), y_c, slice(None), pl.ds(4, 4)))

    for u in range(SUPER):
        for r in range(ROWS):
            wide = gat[(r, *in_super(u))].reshape(EXP, CH).astype(BF)
            both = dot(collapse_ref[...], wide, NN).astype(BF)
            new = dot(both, w_out_ref[...], NN).astype(BF)
            upd[2 * u, r] = new[:TILE]
            upd[2 * u + 1, r] = new[TILE:]

    if starting:
        for d in range(1, n_peer):
            j = peer(d)
            copy = send(
                upd.at[j], ret.at[pl.ds(take * me, take)], r_send.at[d], r_recv.at[me], peer_place(j, c)
            )
            copy.start()
            sends.append(copy)
        ret[pl.ds(take * me, take)] = upd[me]
        for d in range(1, n_peer):
            j = peer(d)
            region = ret.at[pl.ds(take * j, take)]
            send(region, region, r_send.at[d], r_recv.at[j], sibling).wait_recv()
    else:
        mine = lax.rem(me // 2, 2) == c
        my_q = 2 * (me // 4) + lax.rem(me, 2)
        back = []
        for q in range(8):
            p = 4 * (q // 2) + 2 * c + q % 2
            for core in (0, 1):
                copy = send(
                    upd.at[q, pl.ds(3 * core, 3)],
                    ret.at[pl.ds(take * me, take)],
                    r_send.at[2 * q + core],
                    r_recv.at[me],
                    peer_place(p, core),
                )
                local = jnp.logical_and(p == me, c == core)

                @pl.when(jnp.logical_not(local))
                def _():
                    copy.start()

                back.append((local, copy))

        @pl.when(mine)
        def _():
            ret[pl.ds(take * me, take)] = upd[my_q, pl.ds(3 * c, 3)]

        for d in range(n_peer):
            j = peer(d)
            region = ret.at[pl.ds(take * j, take)]
            come = send(region, region, r_send.at[d], r_recv.at[j], sibling)
            if d == 0:

                @pl.when(jnp.logical_not(mine))
                def _():
                    come.wait_recv()

            else:
                come.wait_recv()
        for local, copy in back:

            @pl.when(jnp.logical_not(local))
            def _():
                copy.wait_send()

    def finish():
        for copy in sends:
            copy.wait_send()

        @pl.when(source)
        def _():
            for d in range(1, 8):
                first(d).wait_send()

        for ring in (a1, b1, a2, b2):
            ring.finish()

    return finish


class Bag:
    pass


def kernel(
    tile_ref,
    mask_smem,
    mask_ref,
    ps_ref,
    bs_ref,
    os_ref,
    pe_ref,
    be_ref,
    oe_ref,
    es_ref,
    cs_ref,
    ee_ref,
    ce_ref,
    head_ref,
    start_ref,
    end_ref,
    nt_start,
    nt_end,
    rows_start,
    rows_end,
    bias_start,
    bias_end,
    ret_start,
    ret_end,
    k_t,
    v_ext,
    q_exp,
    g_exp,
    gat,
    upd,
    *sems,
):
    at = here()
    xh, z, xl, y, c = (at[a] for a in AXES)
    x = 2 * xh + xl
    narrow_me, wide_me = xl * 4 + y, xh * 8 + z
    partners = [place(at, c=1 - c)]
    for d in range(1, 8):
        j = lax.rem(narrow_me + d, 8)
        partners.append(place(at, xl=j // 4, y=lax.rem(j, 4)))
    for d in range(1, 16):
        j = lax.rem(wide_me + d, 16)
        for core in (c, 1 - c):
            partners.append(place(at, xh=j // 8, z=lax.rem(j, 8), c=core))
    far = lax.rem(x + jnp.where(xl == 0, 3, 1), 4)
    partners.append(place(at, xh=far // 2, xl=lax.rem(far, 2)))
    barrier = pltpu.get_barrier_semaphore()
    for partner in partners:
        pl.semaphore_signal(barrier, inc=1, device_id=partner, device_id_type=pl.DeviceIdType.MESH)

    b = Bag()
    b.k_t, b.v_ext, b.upd = k_t, v_ext, upd
    b.q_exp, b.g_exp, b.gat = q_exp, g_exp, gat
    key_ok = mask_ref[...].reshape(1, N)
    b.given = {
        True: (mask_smem, key_ok, ps_ref, bs_ref, os_ref, es_ref, cs_ref, head_ref),
        False: (mask_smem, key_ok, pe_ref, be_ref, oe_ref, ee_ref, ce_ref, head_ref),
    }
    half = len(sems) // 2

    nt_start[...] = layer_norm(tile_ref[...].astype(F32))
    finish_start = run(
        True, b, lambda: pl.semaphore_wait(barrier, len(partners)), nt_start, rows_start, bias_start, ret_start, sems[:half]
    )
    update = ret_start[...]
    start_ref[...] = update
    normed = layer_norm(tile_ref[...].astype(F32) + update.astype(F32))
    nt_end[...] = jnp.swapaxes(normed.astype(F32), 0, 1).astype(BF)
    finish_start()
    finish_end = run(False, b, lambda: None, nt_end, rows_end, bias_end, ret_end, sems[half:])
    end_ref[...] = jnp.swapaxes(ret_end[...].astype(F32), 0, 1).astype(BF)
    finish_end()


def expansion(starting):
    row = np.arange(EXP)
    if starting:
        blk, slot, r = row // 192, row % 192 // 24, row % 6
        pos = blk * TILE + 6 * slot + r
    else:
        slot, r6 = row // 24, row % 6
        pos = (r6 // 3) * TILE + 3 * slot + r6 % 3
    expand = (pos[:, None] == np.arange(POS)[None, :]).astype(np.float32)
    head = (row // 6 % HEADS)[:, None] == (np.arange(CH) // DIM)[None, :]
    return expand, head.astype(np.float32)


def on_device(pair_act, mask, w_proj_start, w_bias_start, w_out_start, w_proj_end, w_bias_end, w_out_end):
    (e_start, head), (e_end, _) = expansion(True), expansion(False)
    vmem = pl.BlockSpec(memory_space=pltpu.VMEM)
    smem = pl.BlockSpec(memory_space=pltpu.SMEM)
    dma = pltpu.SemaphoreType.DMA
    tile = pltpu.VMEM((TILE, TILE, CH), BF)
    rows = pltpu.VMEM((16, ROWS, TILE, CH), BF)
    wide_rows = pltpu.VMEM((ROWS, 64, 24, CH), F32)
    sems = [dma((16,)) for _ in range(4)] + [dma((8,)) for _ in range(2)] + [dma((16,)) for _ in range(4)]
    return pl.pallas_call(
        kernel,
        out_shape=[jax.ShapeDtypeStruct((TILE, TILE, CH), BF)] * 2,
        in_specs=[vmem, smem] + [vmem] * 12,
        out_specs=[vmem, vmem],
        scratch_shapes=[
            tile,
            tile,
            rows,
            rows,
            pltpu.VMEM((2, 4, 2, 4, 24, N), F32),
            pltpu.VMEM((2, 2, 2, 8, 24, N), F32),
            tile,
            tile,
            pltpu.VMEM((ROWS, CH, N), BF),
            pltpu.VMEM((ROWS, N, 2 * CH), BF),
            wide_rows,
            wide_rows,
            wide_rows,
            pltpu.VMEM((8, ROWS, TILE, CH), BF),
        ]
        + sems
        + sems,
        compiler_params=pltpu.CompilerParams(
            collective_id=0, has_side_effects=True, vmem_limit_bytes=56 * 1024 * 1024
        ),
        name="triangle_attention",
    )(
        pair_act,
        mask,
        mask,
        w_proj_start,
        w_bias_start.T,
        w_out_start,
        w_proj_end,
        w_bias_end.T,
        w_out_end,
        jnp.asarray(e_start, BF),
        jnp.asarray(e_start.T, BF),
        jnp.asarray(e_end, BF),
        jnp.asarray(e_end.T, BF),
        jnp.asarray(head, F32),
    )


def solution(mesh):
    split = Mesh(mesh.devices.reshape(SIZES), AXES)
    placed = (P(WIDE, NARROW, None),) + (P(),) * 7
    return jax.shard_map(
        on_device,
        mesh=split,
        in_specs=placed,
        out_specs=(P(WIDE, NARROW, None), P(WIDE, NARROW, None)),
        check_vma=False,
    )
```

```python
import functools
import math

import jax
import jax.numpy as jnp
import numpy as np
from jax import lax
from jax.experimental import pallas as pl
from jax.experimental.pallas import tpu as pltpu
from jax.sharding import Mesh
from jax.sharding import PartitionSpec as P

AXES = ("xh", "z", "xl", "y", "c")
SIZES = (2, 8, 2, 4, 2)
NARROW = ("xl", "y", "c")
WIDE = ("xh", "z")

HEADS = 4
DIM = 32
CH = HEADS * DIM
TILE = 48
N = 768
ROWS = 6
SUPER = 4
POS = 2 * TILE
EXP = POS * HEADS
SUB = 192
WAVES = (pl.ds(0, 8), pl.ds(8, 16))
NORM_EPS = 1e-05
MASKED = -1000000000.0
INV_ROOT = DIM ** (-0.5)
ROOT = math.sqrt(DIM)
LOG2E = math.log2(math.e)
BF = jnp.bfloat16
F32 = jnp.float32


def layer_norm(features):
    average = jnp.mean(features, axis=-1, keepdims=True)
    centred = features - average
    spread = jnp.mean(centred * centred, axis=-1, keepdims=True)
    return (centred * lax.rsqrt(spread + NORM_EPS)).astype(BF)


def here():
    return {a: lax.axis_index(a) for a in AXES}


def place(at, **kw):
    return tuple(kw.get(a, at[a]) for a in AXES)


def dot(a, b, dims):
    return lax.dot_general(a, b, (dims, ((), ())), preferred_element_type=F32)


NN = ((1,), (0,))
NT = ((1,), (1,))


def send(src, dst, ssem, rsem, device):
    return pltpu.make_async_remote_copy(
        src_ref=src,
        dst_ref=dst,
        send_sem=ssem,
        recv_sem=rsem,
        device_id=device,
        device_id_type=pl.DeviceIdType.MESH,
    )


class Ring:
    def __init__(self, n, idx, whole, halves, plus, minus, ssem, rsem, base, has=None):
        self.n, self.idx, self.has = n, idx, has
        self.whole, self.halves = whole, halves
        self.plus, self.minus = plus, minus
        self.ssem, self.rsem, self.base = ssem, rsem, base

    def block(self, offset):
        return lax.rem(self.idx + offset + self.n, self.n)

    def copy(self, step, way, block):
        region = self.halves(block)[way] if 2 * step == self.n else self.whole(block)
        at = self.base + 2 * (step - 1) + way
        return send(region, region, self.ssem.at[at], self.rsem.at[at], self.minus if way else self.plus)

    def where(self, block, do):
        if self.has is None:
            do()
        else:
            pl.when(self.has(block))(do)

    def start(self):
        for way in (0, 1):
            self.where(self.idx, lambda: self.copy(1, way, self.idx).start())

    def advance(self, step):
        for way in (0, 1):
            came = self.block(step if way else -step)

            def do():
                self.copy(step, way, came).wait_recv()
                if 2 * step < self.n:
                    self.copy(step + 1, way, came).start()

            self.where(came, do)

    def finish(self):
        for step in range(1, self.n // 2 + 1):
            for way in (0, 1):
                block = self.block(step - 1 if way else 1 - step)
                self.where(block, lambda: self.copy(step, way, block).wait_send())


def picker(offset, transposed):
    shape = (CH, 4 * CH) if transposed else (4 * CH, CH)
    d = lax.broadcasted_iota(jnp.int32, shape, 0 if transposed else 1)
    x = lax.broadcasted_iota(jnp.int32, shape, 1 if transposed else 0)
    return jnp.where(x == (d >> 5) * CH + offset * DIM + (d & 31), 1.0, 0.0).astype(BF)


def run(starting, b, barrier_done, out_tile, rows, bias, ret, sems):
    mask_smem, key_ok, w_proj_ref, w_bias_ref, w_out_ref, expand_ref, collapse_ref, head_ref = b.given[starting]
    k_t, v_ext, upd = b.k_t, b.v_ext, b.upd
    q_exp, g_exp, gat = (ref.reshape(ROWS, *bias.shape[:-1], CH) for ref in (b.q_exp, b.g_exp, b.gat))
    a_send, a_recv, f_send, f_recv, p_send, p_recv, g_send, g_recv, r_send, r_recv = sems
    at = here()
    xh, z, xl, y, c = (at[a] for a in AXES)
    x = 2 * xh + xl
    other = 1 - c
    if starting:
        n_peer, take = 8, 6
        me = xl * 4 + y
        peer_place = lambda j, core: place(at, xl=j // 4, y=lax.rem(j, 4), c=core)
        slot = lambda j, core: (2 * j + core, slice(None))
    else:
        n_peer, take = 16, 3
        me = xh * 8 + z
        peer_place = lambda j, core: place(at, xh=j // 8, z=lax.rem(j, 8), c=core)
        slot = lambda j, core: (j, pl.ds(3 * core, 3))

    def peer(d):
        return lax.rem(me + d, n_peer)

    def x_place(step):
        to = lax.rem(x + step + 4, 4)
        return place(at, xh=to // 2, xl=lax.rem(to, 2))

    y_place = lambda step: place(at, y=lax.rem(y + step + 4, 4))
    z_place = lambda step: place(at, z=lax.rem(z + step + 8, 8))
    sibling = place(at, c=other)

    own = out_tile[pl.ds(take * me, take)]
    rows[slot(me, c)] = own
    barrier_done()

    sends = []
    for d in range(1, n_peer):
        j = peer(d)
        copy = send(
            out_tile.at[pl.ds(take * j, take)],
            rows.at[slot(me, c)],
            a_send.at[d],
            a_recv.at[me],
            peer_place(j, c),
        )
        copy.start()
        sends.append(copy)

    def forward(d):
        j = peer(d)
        region = rows.at[slot(j, c)]
        copy = send(region, region, f_send.at[d], f_recv.at[j], sibling)
        copy.start()
        sends.append(copy)

    forward(0)

    w_all = w_proj_ref[...]
    w_kt = dot(picker(1, True), w_all, NT).astype(BF)
    w_v = dot(w_all, picker(2, False), NN).astype(BF)
    w_qg = jnp.concatenate([dot(w_all, picker(0, False), NN), dot(w_all, picker(3, False), NN)], axis=1).astype(BF)
    s_row = lax.broadcasted_iota(jnp.int32, (24, HEADS), 0)
    s_head = lax.broadcasted_iota(jnp.int32, (24, HEADS), 1)
    w_bias = w_bias_ref[...]
    w_rows = [
        dot(jnp.where(s_row == s_head * ROWS + r, 1.0, 0.0).astype(BF), w_bias, NN).astype(BF) for r in range(ROWS)
    ]

    for d in range(1, n_peer):
        j = peer(d)
        region = rows.at[slot(j, c)]
        send(region, region, a_send.at[d], a_recv.at[j], sibling).wait_recv()
        forward(d)
    for d in range(n_peer):
        j = peer(d)
        region = rows.at[slot(j, other)]
        send(region, region, f_send.at[d], f_recv.at[j], sibling).wait_recv()

    piece = jnp.zeros((24, N), F32)
    for r in range(ROWS):
        piece += dot(w_rows[r], rows[:, r].reshape(N, CH), NT)
    piece = jnp.where(key_ok > 0, piece * ROOT, MASKED)
    y2 = y // 2
    if starting:
        source = lax.rem(z, 2) == c
        own_piece = bias.at[xh, z // 2, xl, y]
        part = lambda k: bias.at[xh, k // 2, xl, y]
        comes = lambda k: jnp.logical_and(lax.rem(k, 2) == c, k != z)
    else:
        source = lax.rem(y, 2) == c
        own_piece = bias.at[xl, y2, xh, z]
        part = lambda k: bias.at[xl, y2, xh, k]
        comes = lambda k: jnp.logical_and(source, k != z)

    def first(w, d):
        region = own_piece.at[WAVES[w]]
        return send(region, region, p_send.at[w, d], p_recv.at[w, z], z_place(d))

    @pl.when(source)
    def _():
        own_piece[...] = piece
        for w in range(len(WAVES)):
            for d in range(1, 8):
                first(w, d).start()

    for r in range(ROWS):
        x_r = rows[:, r].reshape(N, CH)
        k_t[r] = dot(w_kt, x_r, NT).astype(BF)
        v_ext[r, :, :CH] = dot(x_r, w_v, NN).astype(BF)
        v_ext[r, :, CH:] = jnp.ones((N, CH), BF)

    def queries(u, r):
        if starting:
            spots = (4 * u + c, 4 * u + 2 + c)
        else:
            spots = (4 * u + 2 * c, 4 * u + 2 * c + 1)
        x_q = jnp.concatenate([rows[spots[0], r], rows[spots[1], r]], axis=0)
        qg = dot(x_q, w_qg, NN).astype(BF)
        big = dot(expand_ref[...], qg, NN)
        q = (big[:, :CH] * head_ref[...]).reshape(*lead, 24, CH)
        g = (jax.nn.sigmoid(big[:, CH:]) * head_ref[...]).reshape(*lead, 24, CH)
        q_exp[(r, *in_super(u))] = q
        g_exp[(r, *in_super(u))] = g

    if starting:
        lead = (2, 2, 4)
        in_super = lambda u: (u // 2, pl.ds(2 * (u % 2), 2))
    else:
        lead = (2, 8)
        in_super = lambda u: (u // 2, u % 2)

    for r in range(ROWS):
        queries(0, r)
        queries(1, r)

    def first_wait(w):
        for k in range(8):

            @pl.when(comes(k))
            def _():
                region = part(k).at[WAVES[w]]
                send(region, region, p_send.at[w, 0], p_recv.at[w, k], sibling).wait_recv()

    x_args = (x_place(1), x_place(-1), g_send, g_recv)
    y_args = (y_place(1), y_place(-1), g_send, g_recv)
    a1, b1, a2, b2 = [], [], [], []
    for w, rw in enumerate(WAVES):
        base = 16 * w
        if starting:
            a1.append(Ring(
                4, y, lambda k, rw=rw: bias.at[xh, pl.ds(0, 2), xl, k, rw],
                lambda k, rw=rw: (bias.at[xh, 0, xl, k, rw], bias.at[xh, 1, xl, k, rw]), *y_args, base,
            ))
            b1.append(Ring(
                4, x, lambda k, rw=rw: bias.at[k // 2, pl.ds(2, 2), lax.rem(k, 2), y, rw],
                lambda k, rw=rw: (bias.at[k // 2, 2, lax.rem(k, 2), y, rw], bias.at[k // 2, 3, lax.rem(k, 2), y, rw]), *x_args, base + 4,
            ))
            a2.append(Ring(
                4, x, lambda k, rw=rw: bias.at[k // 2, pl.ds(0, 2), lax.rem(k, 2), slice(None), rw],
                lambda k, rw=rw: (bias.at[k // 2, 0, lax.rem(k, 2), slice(None), rw], bias.at[k // 2, 1, lax.rem(k, 2), slice(None), rw]), *x_args, base + 8,
            ))
            b2.append(Ring(
                4, y, lambda k, rw=rw: bias.at[:, pl.ds(2, 2), :, k, rw],
                lambda k, rw=rw: (bias.at[:, 2, :, k, rw], bias.at[:, 3, :, k, rw]), *y_args, base + 12,
            ))
        else:
            has = lambda k: lax.rem(k, 2) == c
            here_only = lambda k: source
            a1.append(Ring(
                4, y, lambda k, rw=rw: bias.at[xl, k // 2, xh, pl.ds(0, 4), rw],
                lambda k, rw=rw: (bias.at[xl, k // 2, xh, pl.ds(0, 2), rw], bias.at[xl, k // 2, xh, pl.ds(2, 2), rw]), *y_args, base, has,
            ))
            b1.append(Ring(
                4, x, lambda k, rw=rw: bias.at[lax.rem(k, 2), y2, k // 2, pl.ds(4, 4), rw],
                lambda k, rw=rw: (
                    bias.at[lax.rem(k, 2), y2, k // 2, pl.ds(4, 2), rw],
                    bias.at[lax.rem(k, 2), y2, k // 2, pl.ds(6, 2), rw],
                ), *x_args, base + 4, here_only,
            ))
            a2.append(Ring(
                4, x, lambda k, rw=rw: bias.at[lax.rem(k, 2), :, k // 2, pl.ds(0, 4), rw],
                lambda k, rw=rw: (
                    bias.at[lax.rem(k, 2), 0, k // 2, pl.ds(0, 4), rw],
                    bias.at[lax.rem(k, 2), 1, k // 2, pl.ds(0, 4), rw],
                ), *x_args, base + 8,
            ))
            b2.append(Ring(
                4, y, lambda k, rw=rw: bias.at[:, k // 2, :, pl.ds(4, 4), rw],
                lambda k, rw=rw: (bias.at[0, k // 2, :, pl.ds(4, 4), rw], bias.at[1, k // 2, :, pl.ds(4, 4), rw]), *y_args, base + 12, has,
            ))

    both = range(len(WAVES))
    def phase_a(w):
        first_wait(w)
        a1[w].start()
        b1[w].start()

    phase_a(0)
    for r in range(ROWS):
        queries(2, r)
    a1[0].advance(1)
    b1[0].advance(1)
    phase_a(1)
    a1[0].advance(2)
    b1[0].advance(2)
    a2[0].start()
    b2[0].start()
    for r in range(ROWS):
        queries(3, r)
    for step in (1, 2):
        a1[1].advance(step)
        b1[1].advance(step)
    a2[1].start()
    b2[1].start()

    if starting:
        line_at = TILE * (8 * xh + z)
        valid = [mask_smem[line_at + ROWS * me + r] for r in range(ROWS)]
    else:
        line_at = TILE * 2 * (4 * xl + y)
        valid = [mask_smem[line_at + TILE * (r // 3) + 3 * me + r % 3] for r in range(ROWS)]
    power = [v.astype(F32) * (INV_ROOT * LOG2E) for v in valid]

    def attend(at):
        pairs = bias[at].reshape(SUB, N)
        for r in range(ROWS):
            t = dot(q_exp[(r, *at)].reshape(SUB, CH).astype(BF), k_t[r], NN) + pairs
            top = jnp.max(t, axis=1, keepdims=True)
            e = jnp.exp2((t - top) * power[r]).astype(BF)
            o = dot(e, v_ext[r], NN)
            gated = g_exp[(r, *at)].reshape(SUB, CH) * (o[:, :CH] / o[:, CH:])
            gat[(r, *at)] = gated.reshape(*q_exp[(r, *at)].shape)

    @pl.loop(0, 4)
    def _(t):
        step = jnp.where(t == 3, 2, jnp.where(t == 2, 3, t))

        @pl.when(t == 1)
        def _():
            for w in both:
                a2[w].advance(1)
                if starting:
                    b2[w].advance(1)

        @pl.when(t == 2)
        def _():
            if not starting:
                for w in both:
                    b2[w].advance(2)

        @pl.when(t == 3)
        def _():
            for w in both:
                a2[w].advance(2)
                if starting:
                    b2[w].advance(2)

        xc = lax.rem(x + step, 4)
        if starting:
            attend((xc // 2, pl.ds(0, 2), lax.rem(xc, 2)))
            attend((slice(None), pl.ds(2, 2), slice(None), lax.rem(y + step, 4)))
        else:
            attend((lax.rem(xc, 2), slice(None), xc // 2, pl.ds(0, 4)))

            @pl.when(t == 0)
            def _():
                for w in both:
                    b2[w].advance(1)

            y_c = jnp.where(t < 2, y2, 1 - y2)
            attend((lax.rem(t, 2), y_c, slice(None), pl.ds(4, 4)))

    for u in range(SUPER):
        for r in range(ROWS):
            wide = gat[(r, *in_super(u))].reshape(EXP, CH).astype(BF)
            joined = dot(collapse_ref[...], wide, NN).astype(BF)
            new = dot(joined, w_out_ref[...], NN).astype(BF)
            upd[2 * u, r] = new[:TILE]
            upd[2 * u + 1, r] = new[TILE:]

    if starting:
        for d in range(1, n_peer):
            j = peer(d)
            copy = send(
                upd.at[j], ret.at[pl.ds(take * me, take)], r_send.at[d], r_recv.at[me], peer_place(j, c)
            )
            copy.start()
            sends.append(copy)
        ret[pl.ds(take * me, take)] = upd[me]
        for d in range(1, n_peer):
            j = peer(d)
            region = ret.at[pl.ds(take * j, take)]
            send(region, region, r_send.at[d], r_recv.at[j], sibling).wait_recv()
    else:
        mine = lax.rem(me // 2, 2) == c
        my_q = 2 * (me // 4) + lax.rem(me, 2)
        back = []
        for q in range(8):
            p = 4 * (q // 2) + 2 * c + q % 2
            for core in (0, 1):
                copy = send(
                    upd.at[q, pl.ds(3 * core, 3)],
                    ret.at[pl.ds(take * me, take)],
                    r_send.at[2 * q + core],
                    r_recv.at[me],
                    peer_place(p, core),
                )
                local = jnp.logical_and(p == me, c == core)

                @pl.when(jnp.logical_not(local))
                def _():
                    copy.start()

                back.append((local, copy))

        @pl.when(mine)
        def _():
            ret[pl.ds(take * me, take)] = upd[my_q, pl.ds(3 * c, 3)]

        for d in range(n_peer):
            j = peer(d)
            region = ret.at[pl.ds(take * j, take)]
            come = send(region, region, r_send.at[d], r_recv.at[j], sibling)
            if d == 0:

                @pl.when(jnp.logical_not(mine))
                def _():
                    come.wait_recv()

            else:
                come.wait_recv()
        for local, copy in back:

            @pl.when(jnp.logical_not(local))
            def _():
                copy.wait_send()

    def finish():
        for copy in sends:
            copy.wait_send()

        @pl.when(source)
        def _():
            for w in both:
                for d in range(1, 8):
                    first(w, d).wait_send()

        for ring in (*a1, *b1, *a2, *b2):
            ring.finish()

    return finish


class Bag:
    pass


def kernel(
    tile_ref,
    mask_smem,
    mask_ref,
    ps_ref,
    bs_ref,
    os_ref,
    pe_ref,
    be_ref,
    oe_ref,
    es_ref,
    cs_ref,
    ee_ref,
    ce_ref,
    head_ref,
    start_ref,
    end_ref,
    nt_start,
    nt_end,
    rows_start,
    rows_end,
    bias_start,
    bias_end,
    ret_start,
    ret_end,
    k_t,
    v_ext,
    q_exp,
    g_exp,
    gat,
    upd,
    *sems,
):
    at = here()
    xh, z, xl, y, c = (at[a] for a in AXES)
    x = 2 * xh + xl
    narrow_me, wide_me = xl * 4 + y, xh * 8 + z
    partners = [place(at, c=1 - c)]
    for d in range(1, 8):
        j = lax.rem(narrow_me + d, 8)
        partners.append(place(at, xl=j // 4, y=lax.rem(j, 4)))
    for d in range(1, 16):
        j = lax.rem(wide_me + d, 16)
        for core in (c, 1 - c):
            partners.append(place(at, xh=j // 8, z=lax.rem(j, 8), c=core))
    far = lax.rem(x + jnp.where(xl == 0, 3, 1), 4)
    partners.append(place(at, xh=far // 2, xl=lax.rem(far, 2)))
    barrier = pltpu.get_barrier_semaphore()
    for partner in partners:
        pl.semaphore_signal(barrier, inc=1, device_id=partner, device_id_type=pl.DeviceIdType.MESH)

    b = Bag()
    b.k_t, b.v_ext, b.upd = k_t, v_ext, upd
    b.q_exp, b.g_exp, b.gat = q_exp, g_exp, gat
    key_ok = mask_ref[...].reshape(1, N)
    b.given = {
        True: (mask_smem, key_ok, ps_ref, bs_ref, os_ref, es_ref, cs_ref, head_ref),
        False: (mask_smem, key_ok, pe_ref, be_ref, oe_ref, ee_ref, ce_ref, head_ref),
    }
    half = len(sems) // 2

    nt_start[...] = layer_norm(tile_ref[...].astype(F32))
    finish_start = run(
        True, b, lambda: pl.semaphore_wait(barrier, len(partners)), nt_start, rows_start, bias_start, ret_start, sems[:half]
    )
    update = ret_start[...]
    start_ref[...] = update
    normed = layer_norm(tile_ref[...].astype(F32) + update.astype(F32))
    nt_end[...] = jnp.swapaxes(normed.astype(F32), 0, 1).astype(BF)
    finish_start()
    finish_end = run(False, b, lambda: None, nt_end, rows_end, bias_end, ret_end, sems[half:])
    end_ref[...] = jnp.swapaxes(ret_end[...].astype(F32), 0, 1).astype(BF)
    finish_end()


def expansion(starting):
    row = np.arange(EXP)
    if starting:
        blk, slot, r = row // 192, row % 192 // 24, row % 6
        pos = blk * TILE + 6 * slot + r
    else:
        slot, r6 = row // 24, row % 6
        pos = (r6 // 3) * TILE + 3 * slot + r6 % 3
    expand = (pos[:, None] == np.arange(POS)[None, :]).astype(np.float32)
    head = (row // 6 % HEADS)[:, None] == (np.arange(CH) // DIM)[None, :]
    return expand, head.astype(np.float32)


def on_device(pair_act, mask, w_proj_start, w_bias_start, w_out_start, w_proj_end, w_bias_end, w_out_end):
    (e_start, head), (e_end, _) = expansion(True), expansion(False)
    vmem = pl.BlockSpec(memory_space=pltpu.VMEM)
    smem = pl.BlockSpec(memory_space=pltpu.SMEM)
    dma = pltpu.SemaphoreType.DMA
    tile = pltpu.VMEM((TILE, TILE, CH), BF)
    rows = pltpu.VMEM((16, ROWS, TILE, CH), BF)
    wide_rows = pltpu.VMEM((ROWS, 64, 24, CH), F32)
    sems = [dma((16,)) for _ in range(4)] + [dma((2, 8)) for _ in range(2)] + [dma((32,)) for _ in range(2)] + [dma((16,)) for _ in range(2)]
    return pl.pallas_call(
        kernel,
        out_shape=[jax.ShapeDtypeStruct((TILE, TILE, CH), BF)] * 2,
        in_specs=[vmem, smem] + [vmem] * 12,
        out_specs=[vmem, vmem],
        scratch_shapes=[
            tile,
            tile,
            rows,
            rows,
            pltpu.VMEM((2, 4, 2, 4, 24, N), F32),
            pltpu.VMEM((2, 2, 2, 8, 24, N), F32),
            tile,
            tile,
            pltpu.VMEM((ROWS, CH, N), BF),
            pltpu.VMEM((ROWS, N, 2 * CH), BF),
            wide_rows,
            wide_rows,
            wide_rows,
            pltpu.VMEM((8, ROWS, TILE, CH), BF),
        ]
        + sems
        + sems,
        compiler_params=pltpu.CompilerParams(
            collective_id=0, has_side_effects=True, vmem_limit_bytes=56 * 1024 * 1024
        ),
        name="triangle_attention",
    )(
        pair_act,
        mask,
        mask,
        w_proj_start,
        w_bias_start.T,
        w_out_start,
        w_proj_end,
        w_bias_end.T,
        w_out_end,
        jnp.asarray(e_start, BF),
        jnp.asarray(e_start.T, BF),
        jnp.asarray(e_end, BF),
        jnp.asarray(e_end.T, BF),
        jnp.asarray(head, F32),
    )


def solution(mesh):
    split = Mesh(mesh.devices.reshape(SIZES), AXES)
    placed = (P(WIDE, NARROW, None),) + (P(),) * 7
    return jax.shard_map(
        on_device,
        mesh=split,
        in_specs=placed,
        out_specs=(P(WIDE, NARROW, None), P(WIDE, NARROW, None)),
        check_vma=False,
    )
```

```python
import functools
import math

import jax
import jax.numpy as jnp
import numpy as np
from jax import lax
from jax.experimental import pallas as pl
from jax.experimental.pallas import tpu as pltpu
from jax.sharding import Mesh
from jax.sharding import PartitionSpec as P

AXES = ("xh", "z", "xl", "y", "c")
SIZES = (2, 8, 2, 4, 2)
NARROW = ("xl", "y", "c")
WIDE = ("xh", "z")

HEADS = 4
DIM = 32
CH = HEADS * DIM
TILE = 48
N = 768
ROWS = 6
SUPER = 4
POS = 2 * TILE
EXP = POS * HEADS
SUB = 192
WAVES = (pl.ds(0, 8), pl.ds(8, 16))
NORM_EPS = 1e-05
MASKED = -1000000000.0
INV_ROOT = DIM ** (-0.5)
ROOT = math.sqrt(DIM)
LOG2E = math.log2(math.e)
BF = jnp.bfloat16
F32 = jnp.float32


def layer_norm(features):
    average = jnp.mean(features, axis=-1, keepdims=True)
    centred = features - average
    spread = jnp.mean(centred * centred, axis=-1, keepdims=True)
    return (centred * lax.rsqrt(spread + NORM_EPS)).astype(BF)


def here():
    return {a: lax.axis_index(a) for a in AXES}


def place(at, **kw):
    return tuple(kw.get(a, at[a]) for a in AXES)


def dot(a, b, dims):
    return lax.dot_general(a, b, (dims, ((), ())), preferred_element_type=F32)


NN = ((1,), (0,))
NT = ((1,), (1,))


def send(src, dst, ssem, rsem, device):
    return pltpu.make_async_remote_copy(
        src_ref=src,
        dst_ref=dst,
        send_sem=ssem,
        recv_sem=rsem,
        device_id=device,
        device_id_type=pl.DeviceIdType.MESH,
    )


class Ring:
    def __init__(self, n, idx, whole, halves, plus, minus, ssem, rsem, base, has=None):
        self.n, self.idx, self.has = n, idx, has
        self.whole, self.halves = whole, halves
        self.plus, self.minus = plus, minus
        self.ssem, self.rsem, self.base = ssem, rsem, base

    def block(self, offset):
        return lax.rem(self.idx + offset + self.n, self.n)

    def copy(self, step, way, block):
        region = self.halves(block)[way] if 2 * step == self.n else self.whole(block)
        at = self.base + 2 * (step - 1) + way
        return send(region, region, self.ssem.at[at], self.rsem.at[at], self.minus if way else self.plus)

    def where(self, block, do):
        if self.has is None:
            do()
        else:
            pl.when(self.has(block))(do)

    def start(self):
        for way in (0, 1):
            self.where(self.idx, lambda: self.copy(1, way, self.idx).start())

    def advance(self, step):
        for way in (0, 1):
            came = self.block(step if way else -step)

            def do():
                self.copy(step, way, came).wait_recv()
                if 2 * step < self.n:
                    self.copy(step + 1, way, came).start()

            self.where(came, do)

    def finish(self):
        for step in range(1, self.n // 2 + 1):
            for way in (0, 1):
                block = self.block(step - 1 if way else 1 - step)
                self.where(block, lambda: self.copy(step, way, block).wait_send())


def picker(offset, transposed):
    shape = (CH, 4 * CH) if transposed else (4 * CH, CH)
    d = lax.broadcasted_iota(jnp.int32, shape, 0 if transposed else 1)
    x = lax.broadcasted_iota(jnp.int32, shape, 1 if transposed else 0)
    return jnp.where(x == (d >> 5) * CH + offset * DIM + (d & 31), 1.0, 0.0).astype(BF)


def run(starting, b, barrier_done, out_tile, rows, bias, ret, sems):
    mask_smem, key_ok, w_proj_ref, w_bias_ref, w_out_ref, expand_ref, collapse_ref, head_ref = b.given[starting]
    k_t, v_ext, upd = b.k_t, b.v_ext, b.upd
    q_exp, g_exp, gat = (ref.reshape(ROWS, *bias.shape[:-1], CH) for ref in (b.q_exp, b.g_exp, b.gat))
    a_send, a_recv, f_send, f_recv, p_send, p_recv, g_send, g_recv, r_send, r_recv = sems
    at = here()
    xh, z, xl, y, c = (at[a] for a in AXES)
    x = 2 * xh + xl
    other = 1 - c
    if starting:
        n_peer, take = 8, 6
        me = xl * 4 + y
        peer_place = lambda j, core: place(at, xl=j // 4, y=lax.rem(j, 4), c=core)
        slot = lambda j, core: (2 * j + core, slice(None))
    else:
        n_peer, take = 16, 3
        me = xh * 8 + z
        peer_place = lambda j, core: place(at, xh=j // 8, z=lax.rem(j, 8), c=core)
        slot = lambda j, core: (j, pl.ds(3 * core, 3))

    def peer(d):
        return lax.rem(me + d, n_peer)

    def x_place(step):
        to = lax.rem(x + step + 4, 4)
        return place(at, xh=to // 2, xl=lax.rem(to, 2))

    y_place = lambda step: place(at, y=lax.rem(y + step + 4, 4))
    z_place = lambda step: place(at, z=lax.rem(z + step + 8, 8))
    sibling = place(at, c=other)

    own = out_tile[pl.ds(take * me, take)]
    rows[slot(me, c)] = own
    barrier_done()

    sends = []
    for d in range(1, n_peer):
        j = peer(d)
        copy = send(
            out_tile.at[pl.ds(take * j, take)],
            rows.at[slot(me, c)],
            a_send.at[d],
            a_recv.at[me],
            peer_place(j, c),
        )
        copy.start()
        sends.append(copy)

    def forward(d):
        j = peer(d)
        region = rows.at[slot(j, c)]
        copy = send(region, region, f_send.at[d], f_recv.at[j], sibling)
        copy.start()
        sends.append(copy)

    forward(0)

    w_all = w_proj_ref[...]
    w_kt = dot(picker(1, True), w_all, NT).astype(BF)
    w_v = dot(w_all, picker(2, False), NN).astype(BF)
    w_qg = jnp.concatenate([dot(w_all, picker(0, False), NN), dot(w_all, picker(3, False), NN)], axis=1).astype(BF)
    s_row = lax.broadcasted_iota(jnp.int32, (24, HEADS), 0)
    s_head = lax.broadcasted_iota(jnp.int32, (24, HEADS), 1)
    w_bias = w_bias_ref[...]
    w_rows = [
        dot(jnp.where(s_row == s_head * ROWS + r, 1.0, 0.0).astype(BF), w_bias, NN).astype(BF) for r in range(ROWS)
    ]

    for d in range(1, n_peer):
        j = peer(d)
        region = rows.at[slot(j, c)]
        send(region, region, a_send.at[d], a_recv.at[j], sibling).wait_recv()
        forward(d)
    for d in range(n_peer):
        j = peer(d)
        region = rows.at[slot(j, other)]
        send(region, region, f_send.at[d], f_recv.at[j], sibling).wait_recv()

    piece = jnp.zeros((24, N), F32)
    for r in range(ROWS):
        piece += dot(w_rows[r], rows[:, r].reshape(N, CH), NT)
    piece = jnp.where(key_ok > 0, piece * ROOT, MASKED)
    y2 = y // 2
    if starting:
        source = lax.rem(z, 2) == c
        own_piece = bias.at[xh, z // 2, xl, y]
        part = lambda k: bias.at[xh, k // 2, xl, y]
        comes = lambda k: jnp.logical_and(lax.rem(k, 2) == c, k != z)
    else:
        source = lax.rem(y, 2) == c
        own_piece = bias.at[xl, y2, xh, z]
        part = lambda k: bias.at[xl, y2, xh, k]
        comes = lambda k: jnp.logical_and(source, k != z)

    def first(w, d):
        region = own_piece.at[WAVES[w]]
        return send(region, region, p_send.at[w, d], p_recv.at[w, z], z_place(d))

    @pl.when(source)
    def _():
        own_piece[...] = piece
        for w in range(len(WAVES)):
            for d in range(1, 8):
                first(w, d).start()

    for r in range(ROWS):
        x_r = rows[:, r].reshape(N, CH)
        k_t[r] = dot(w_kt, x_r, NT).astype(BF)
        v_ext[r, :, :CH] = dot(x_r, w_v, NN).astype(BF)
        v_ext[r, :, CH:] = jnp.ones((N, CH), BF)

    def queries(u, r):
        if starting:
            spots = (4 * u + c, 4 * u + 2 + c)
        else:
            spots = (4 * u + 2 * c, 4 * u + 2 * c + 1)
        x_q = jnp.concatenate([rows[spots[0], r], rows[spots[1], r]], axis=0)
        qg = dot(x_q, w_qg, NN).astype(BF)
        big = dot(expand_ref[...], qg, NN)
        q = (big[:, :CH] * head_ref[...]).reshape(*lead, 24, CH)
        g = (jax.nn.sigmoid(big[:, CH:]) * head_ref[...]).reshape(*lead, 24, CH)
        q_exp[(r, *in_super(u))] = q
        g_exp[(r, *in_super(u))] = g

    if starting:
        lead = (2, 2, 4)
        in_super = lambda u: (u // 2, pl.ds(2 * (u % 2), 2))
    else:
        lead = (2, 8)
        in_super = lambda u: (u // 2, u % 2)

    for r in range(ROWS):
        queries(0, r)
    def first_wait(w):
        for k in range(8):

            @pl.when(comes(k))
            def _():
                region = part(k).at[WAVES[w]]
                send(region, region, p_send.at[w, 0], p_recv.at[w, k], sibling).wait_recv()

    x_args = (x_place(1), x_place(-1), g_send, g_recv)
    y_args = (y_place(1), y_place(-1), g_send, g_recv)
    a1, b1, a2, b2 = [], [], [], []
    for w, rw in enumerate(WAVES):
        base = 16 * w
        if starting:
            a1.append(Ring(
                4, y, lambda k, rw=rw: bias.at[xh, pl.ds(0, 2), xl, k, rw],
                lambda k, rw=rw: (bias.at[xh, 0, xl, k, rw], bias.at[xh, 1, xl, k, rw]), *y_args, base,
            ))
            b1.append(Ring(
                4, x, lambda k, rw=rw: bias.at[k // 2, pl.ds(2, 2), lax.rem(k, 2), y, rw],
                lambda k, rw=rw: (bias.at[k // 2, 2, lax.rem(k, 2), y, rw], bias.at[k // 2, 3, lax.rem(k, 2), y, rw]), *x_args, base + 4,
            ))
            a2.append(Ring(
                4, x, lambda k, rw=rw: bias.at[k // 2, pl.ds(0, 2), lax.rem(k, 2), slice(None), rw],
                lambda k, rw=rw: (bias.at[k // 2, 0, lax.rem(k, 2), slice(None), rw], bias.at[k // 2, 1, lax.rem(k, 2), slice(None), rw]), *x_args, base + 8,
            ))
            b2.append(Ring(
                4, y, lambda k, rw=rw: bias.at[:, pl.ds(2, 2), :, k, rw],
                lambda k, rw=rw: (bias.at[:, 2, :, k, rw], bias.at[:, 3, :, k, rw]), *y_args, base + 12,
            ))
        else:
            has = lambda k: lax.rem(k, 2) == c
            here_only = lambda k: source
            a1.append(Ring(
                4, y, lambda k, rw=rw: bias.at[xl, k // 2, xh, pl.ds(0, 4), rw],
                lambda k, rw=rw: (bias.at[xl, k // 2, xh, pl.ds(0, 2), rw], bias.at[xl, k // 2, xh, pl.ds(2, 2), rw]), *y_args, base, has,
            ))
            b1.append(Ring(
                4, x, lambda k, rw=rw: bias.at[lax.rem(k, 2), y2, k // 2, pl.ds(4, 4), rw],
                lambda k, rw=rw: (
                    bias.at[lax.rem(k, 2), y2, k // 2, pl.ds(4, 2), rw],
                    bias.at[lax.rem(k, 2), y2, k // 2, pl.ds(6, 2), rw],
                ), *x_args, base + 4, here_only,
            ))
            a2.append(Ring(
                4, x, lambda k, rw=rw: bias.at[lax.rem(k, 2), :, k // 2, pl.ds(0, 4), rw],
                lambda k, rw=rw: (
                    bias.at[lax.rem(k, 2), 0, k // 2, pl.ds(0, 4), rw],
                    bias.at[lax.rem(k, 2), 1, k // 2, pl.ds(0, 4), rw],
                ), *x_args, base + 8,
            ))
            b2.append(Ring(
                4, y, lambda k, rw=rw: bias.at[:, k // 2, :, pl.ds(4, 4), rw],
                lambda k, rw=rw: (bias.at[0, k // 2, :, pl.ds(4, 4), rw], bias.at[1, k // 2, :, pl.ds(4, 4), rw]), *y_args, base + 12, has,
            ))

    both = range(len(WAVES))
    def phase_a(w):
        first_wait(w)
        a1[w].start()
        b1[w].start()

    phase_a(0)
    for r in range(ROWS):
        queries(1, r)
    a1[0].advance(1)
    b1[0].advance(1)
    phase_a(1)
    a1[0].advance(2)
    b1[0].advance(2)
    a2[0].start()
    b2[0].start()
    for step in (1, 2):
        a1[1].advance(step)
        b1[1].advance(step)
    a2[1].start()
    b2[1].start()
    for r in range(ROWS):
        queries(2, r)
        queries(3, r)

    if starting:
        line_at = TILE * (8 * xh + z)
        valid = [mask_smem[line_at + ROWS * me + r] for r in range(ROWS)]
    else:
        line_at = TILE * 2 * (4 * xl + y)
        valid = [mask_smem[line_at + TILE * (r // 3) + 3 * me + r % 3] for r in range(ROWS)]
    power = [v.astype(F32) * (INV_ROOT * LOG2E) for v in valid]

    def attend(at):
        pairs = bias[at].reshape(SUB, N)
        for r in range(ROWS):
            t = dot(q_exp[(r, *at)].reshape(SUB, CH).astype(BF), k_t[r], NN) + pairs
            top = jnp.max(t, axis=1, keepdims=True)
            e = jnp.exp2((t - top) * power[r]).astype(BF)
            o = dot(e, v_ext[r], NN)
            gated = g_exp[(r, *at)].reshape(SUB, CH) * (o[:, :CH] / o[:, CH:])
            gat[(r, *at)] = gated.reshape(*q_exp[(r, *at)].shape)

    def collapse(u):
        for r in range(ROWS):
            wide = gat[(r, *in_super(u))].reshape(EXP, CH).astype(BF)
            joined = dot(collapse_ref[...], wide, NN).astype(BF)
            new = dot(joined, w_out_ref[...], NN).astype(BF)
            upd[2 * u, r] = new[:TILE]
            upd[2 * u + 1, r] = new[TILE:]

    back_to = ret.at[pl.ds(take * me, take)]

    def backs(u, at):
        for blk in (0, 1):
            q = 2 * u + blk
            if starting:
                yield q != me, send(upd.at[q], back_to, r_send.at[2 * at + blk], r_recv.at[me], peer_place(q, c))
            else:
                p = 4 * u + 2 * c + blk
                for core in (0, 1):
                    yield jnp.logical_or(p != me, c != core), send(
                        upd.at[q, pl.ds(3 * core, 3)],
                        back_to,
                        r_send.at[4 * at + 2 * blk + core],
                        r_recv.at[me],
                        peer_place(p, core),
                    )

    def give(u, at):
        collapse(u)
        for other_device, copy in backs(u, at):
            pl.when(other_device)(copy.start)

    done = (0, 2, 1, 3) if starting else (2 - 2 * xl, 3 - 2 * xl, 2 * xl, 2 * xl + 1)

    @pl.loop(0, 8)
    def _(h):
        t = h // 2
        step = jnp.where(t == 3, 2, jnp.where(t == 2, 3, t))
        first_kind = lax.rem(h, 2) == 0
        if not starting:
            first_kind = jnp.where(h < 6, lax.rem(h, 2), 7 - h) == 0
        rings = {1: [], 2: [], 5: [], 6: [], 7: []}
        if starting:
            rings[2] = [(a2, 1), (b2, 1)]
            rings[6] = [(a2, 2), (b2, 2)]
        else:
            rings[1] = [(b2, 1)]
            rings[2] = [(a2, 1)]
            rings[5] = [(b2, 2)]
            rings[7] = [(a2, 2)]
        for when, moves in rings.items():
            if moves:

                @pl.when(h == when)
                def _():
                    for ring, move in moves:
                        for w in both:
                            ring[w].advance(move)

        xc = lax.rem(x + step, 4)

        @pl.when(first_kind)
        def _():
            if starting:
                attend((xc // 2, pl.ds(0, 2), lax.rem(xc, 2)))
            else:
                attend((lax.rem(xc, 2), slice(None), xc // 2, pl.ds(0, 4)))

        @pl.when(jnp.logical_not(first_kind))
        def _():
            if starting:
                attend((slice(None), pl.ds(2, 2), slice(None), lax.rem(y + step, 4)))
            else:
                y_c = jnp.where(t < 2, y2, 1 - y2)
                attend((lax.rem(t, 2), y_c, slice(None), pl.ds(4, 4)))

        @pl.when(h == 6)
        def _():
            give(done[0], 0)
            give(done[1], 1)

    give(done[2], 2)
    give(done[3], 3)
    if starting:
        back_to[...] = upd[me]
    else:
        mine = lax.rem(me // 2, 2) == c

        @pl.when(mine)
        def _():
            back_to[...] = upd[2 * (me // 4) + lax.rem(me, 2), pl.ds(3 * c, 3)]

    for d in range(n_peer):
        j = peer(d)
        region = ret.at[pl.ds(take * j, take)]
        come = send(region, region, r_send.at[d], r_recv.at[j], sibling)
        if d:
            come.wait_recv()
        elif not starting:
            pl.when(jnp.logical_not(mine))(come.wait_recv)

    def finish():
        for copy in sends:
            copy.wait_send()
        for at, u in enumerate(done):
            for other_device, copy in backs(u, at):
                pl.when(other_device)(copy.wait_send)

        @pl.when(source)
        def _():
            for w in both:
                for d in range(1, 8):
                    first(w, d).wait_send()

        for ring in (*a1, *b1, *a2, *b2):
            ring.finish()

    return finish


class Bag:
    pass


def kernel(
    tile_ref,
    mask_smem,
    mask_ref,
    ps_ref,
    bs_ref,
    os_ref,
    pe_ref,
    be_ref,
    oe_ref,
    es_ref,
    cs_ref,
    ee_ref,
    ce_ref,
    head_ref,
    start_ref,
    end_ref,
    nt_start,
    nt_end,
    rows_start,
    rows_end,
    bias_start,
    bias_end,
    ret_start,
    ret_end,
    k_t,
    v_ext,
    q_exp,
    g_exp,
    gat,
    upd,
    *sems,
):
    at = here()
    xh, z, xl, y, c = (at[a] for a in AXES)
    x = 2 * xh + xl
    narrow_me, wide_me = xl * 4 + y, xh * 8 + z
    partners = [place(at, c=1 - c)]
    for d in range(1, 8):
        j = lax.rem(narrow_me + d, 8)
        partners.append(place(at, xl=j // 4, y=lax.rem(j, 4)))
    for d in range(1, 16):
        j = lax.rem(wide_me + d, 16)
        for core in (c, 1 - c):
            partners.append(place(at, xh=j // 8, z=lax.rem(j, 8), c=core))
    far = lax.rem(x + jnp.where(xl == 0, 3, 1), 4)
    partners.append(place(at, xh=far // 2, xl=lax.rem(far, 2)))
    barrier = pltpu.get_barrier_semaphore()
    for partner in partners:
        pl.semaphore_signal(barrier, inc=1, device_id=partner, device_id_type=pl.DeviceIdType.MESH)

    b = Bag()
    b.k_t, b.v_ext, b.upd = k_t, v_ext, upd
    b.q_exp, b.g_exp, b.gat = q_exp, g_exp, gat
    key_ok = mask_ref[...].reshape(1, N)
    b.given = {
        True: (mask_smem, key_ok, ps_ref, bs_ref, os_ref, es_ref, cs_ref, head_ref),
        False: (mask_smem, key_ok, pe_ref, be_ref, oe_ref, ee_ref, ce_ref, head_ref),
    }
    half = len(sems) // 2

    nt_start[...] = layer_norm(tile_ref[...].astype(F32))
    finish_start = run(
        True, b, lambda: pl.semaphore_wait(barrier, len(partners)), nt_start, rows_start, bias_start, ret_start, sems[:half]
    )
    update = ret_start[...]
    start_ref[...] = update
    normed = layer_norm(tile_ref[...].astype(F32) + update.astype(F32))
    nt_end[...] = jnp.swapaxes(normed.astype(F32), 0, 1).astype(BF)
    finish_start()
    finish_end = run(False, b, lambda: None, nt_end, rows_end, bias_end, ret_end, sems[half:])
    end_ref[...] = jnp.swapaxes(ret_end[...].astype(F32), 0, 1).astype(BF)
    finish_end()


def expansion(starting):
    row = np.arange(EXP)
    if starting:
        blk, slot, r = row // 192, row % 192 // 24, row % 6
        pos = blk * TILE + 6 * slot + r
    else:
        slot, r6 = row // 24, row % 6
        pos = (r6 // 3) * TILE + 3 * slot + r6 % 3
    expand = (pos[:, None] == np.arange(POS)[None, :]).astype(np.float32)
    head = (row // 6 % HEADS)[:, None] == (np.arange(CH) // DIM)[None, :]
    return expand, head.astype(np.float32)


def on_device(pair_act, mask, w_proj_start, w_bias_start, w_out_start, w_proj_end, w_bias_end, w_out_end):
    (e_start, head), (e_end, _) = expansion(True), expansion(False)
    vmem = pl.BlockSpec(memory_space=pltpu.VMEM)
    smem = pl.BlockSpec(memory_space=pltpu.SMEM)
    dma = pltpu.SemaphoreType.DMA
    tile = pltpu.VMEM((TILE, TILE, CH), BF)
    rows = pltpu.VMEM((16, ROWS, TILE, CH), BF)
    wide_rows = pltpu.VMEM((ROWS, 64, 24, CH), F32)
    sems = [dma((16,)) for _ in range(4)] + [dma((2, 8)) for _ in range(2)] + [dma((32,)) for _ in range(2)] + [dma((16,)) for _ in range(2)]
    return pl.pallas_call(
        kernel,
        out_shape=[jax.ShapeDtypeStruct((TILE, TILE, CH), BF)] * 2,
        in_specs=[vmem, smem] + [vmem] * 12,
        out_specs=[vmem, vmem],
        scratch_shapes=[
            tile,
            tile,
            rows,
            rows,
            pltpu.VMEM((2, 4, 2, 4, 24, N), F32),
            pltpu.VMEM((2, 2, 2, 8, 24, N), F32),
            tile,
            tile,
            pltpu.VMEM((ROWS, CH, N), BF),
            pltpu.VMEM((ROWS, N, 2 * CH), BF),
            wide_rows,
            wide_rows,
            wide_rows,
            pltpu.VMEM((8, ROWS, TILE, CH), BF),
        ]
        + sems
        + sems,
        compiler_params=pltpu.CompilerParams(
            collective_id=0, has_side_effects=True, vmem_limit_bytes=56 * 1024 * 1024
        ),
        name="triangle_attention",
    )(
        pair_act,
        mask,
        mask,
        w_proj_start,
        w_bias_start.T,
        w_out_start,
        w_proj_end,
        w_bias_end.T,
        w_out_end,
        jnp.asarray(e_start, BF),
        jnp.asarray(e_start.T, BF),
        jnp.asarray(e_end, BF),
        jnp.asarray(e_end.T, BF),
        jnp.asarray(head, F32),
    )


def solution(mesh):
    split = Mesh(mesh.devices.reshape(SIZES), AXES)
    placed = (P(WIDE, NARROW, None),) + (P(),) * 7
    return jax.shard_map(
        on_device,
        mesh=split,
        in_specs=placed,
        out_specs=(P(WIDE, NARROW, None), P(WIDE, NARROW, None)),
        check_vma=False,
    )
```

```python
import functools
import math

import jax
import jax.numpy as jnp
import numpy as np
from jax import lax
from jax.experimental import pallas as pl
from jax.experimental.pallas import tpu as pltpu
from jax.sharding import Mesh
from jax.sharding import PartitionSpec as P

AXES = ("xh", "z", "xl", "y", "c")
SIZES = (2, 8, 2, 4, 2)
NARROW = ("xl", "y", "c")
WIDE = ("xh", "z")

HEADS = 4
DIM = 32
CH = HEADS * DIM
TILE = 48
N = 768
ROWS = 6
SUPER = 4
POS = 2 * TILE
EXP = POS * HEADS
SUB = 192
WAVES = (pl.ds(0, 8), pl.ds(8, 16))
NORM_EPS = 1e-05
MASKED = -1000000000.0
INV_ROOT = DIM ** (-0.5)
ROOT = math.sqrt(DIM)
LOG2E = math.log2(math.e)
BF = jnp.bfloat16
F32 = jnp.float32


def layer_norm(features):
    average = jnp.mean(features, axis=-1, keepdims=True)
    centred = features - average
    spread = jnp.mean(centred * centred, axis=-1, keepdims=True)
    return (centred * lax.rsqrt(spread + NORM_EPS)).astype(BF)


def here():
    return {a: lax.axis_index(a) for a in AXES}


def place(at, **kw):
    return tuple(kw.get(a, at[a]) for a in AXES)


def dot(a, b, dims):
    return lax.dot_general(a, b, (dims, ((), ())), preferred_element_type=F32)


NN = ((1,), (0,))
NT = ((1,), (1,))


def send(src, dst, ssem, rsem, device):
    return pltpu.make_async_remote_copy(
        src_ref=src,
        dst_ref=dst,
        send_sem=ssem,
        recv_sem=rsem,
        device_id=device,
        device_id_type=pl.DeviceIdType.MESH,
    )


class Ring:
    def __init__(self, n, idx, whole, halves, plus, minus, ssem, rsem, base, has=None):
        self.n, self.idx, self.has = n, idx, has
        self.whole, self.halves = whole, halves
        self.plus, self.minus = plus, minus
        self.ssem, self.rsem, self.base = ssem, rsem, base

    def block(self, offset):
        return lax.rem(self.idx + offset + self.n, self.n)

    def copy(self, step, way, block):
        region = self.halves(block)[way] if 2 * step == self.n else self.whole(block)
        at = self.base + 2 * (step - 1) + way
        return send(region, region, self.ssem.at[at], self.rsem.at[at], self.minus if way else self.plus)

    def where(self, block, do):
        if self.has is None:
            do()
        else:
            pl.when(self.has(block))(do)

    def start(self):
        for way in (0, 1):
            self.where(self.idx, lambda: self.copy(1, way, self.idx).start())

    def advance(self, step):
        for way in (0, 1):
            came = self.block(step if way else -step)

            def do():
                self.copy(step, way, came).wait_recv()
                if 2 * step < self.n:
                    self.copy(step + 1, way, came).start()

            self.where(came, do)

    def finish(self):
        for step in range(1, self.n // 2 + 1):
            for way in (0, 1):
                block = self.block(step - 1 if way else 1 - step)
                self.where(block, lambda: self.copy(step, way, block).wait_send())


def picker(offset, transposed):
    shape = (CH, 4 * CH) if transposed else (4 * CH, CH)
    d = lax.broadcasted_iota(jnp.int32, shape, 0 if transposed else 1)
    x = lax.broadcasted_iota(jnp.int32, shape, 1 if transposed else 0)
    return jnp.where(x == (d >> 5) * CH + offset * DIM + (d & 31), 1.0, 0.0).astype(BF)


def run(starting, b, barrier_done, out_tile, rows, bias, ret, sems):
    mask_smem, key_ok, w_proj_ref, w_bias_ref, w_out_ref, expand_ref, collapse_ref, head_ref = b.given[starting]
    k_t, v_ext, upd = b.k_t, b.v_ext, b.upd
    q_exp, g_exp, gat = (ref.reshape(ROWS, *bias.shape[:-1], CH) for ref in (b.q_exp, b.g_exp, b.gat))
    a_send, a_recv, f_send, f_recv, p_send, p_recv, g_send, g_recv, r_send, r_recv = sems
    at = here()
    xh, z, xl, y, c = (at[a] for a in AXES)
    x = 2 * xh + xl
    other = 1 - c
    if starting:
        n_peer, take = 8, 6
        me = xl * 4 + y
        peer_place = lambda j, core: place(at, xl=j // 4, y=lax.rem(j, 4), c=core)
        slot = lambda j, core: (2 * j + core, slice(None))
    else:
        n_peer, take = 16, 3
        me = xh * 8 + z
        peer_place = lambda j, core: place(at, xh=j // 8, z=lax.rem(j, 8), c=core)
        slot = lambda j, core: (j, pl.ds(3 * core, 3))

    def peer(d):
        return lax.rem(me + d, n_peer)

    def x_place(step):
        to = lax.rem(x + step + 4, 4)
        return place(at, xh=to // 2, xl=lax.rem(to, 2))

    y_place = lambda step: place(at, y=lax.rem(y + step + 4, 4))
    z_place = lambda step: place(at, z=lax.rem(z + step + 8, 8))
    sibling = place(at, c=other)

    own = out_tile[pl.ds(take * me, take)]
    rows[slot(me, c)] = own
    barrier_done()

    sends = []
    for d in range(1, n_peer):
        j = peer(d)
        copy = send(
            out_tile.at[pl.ds(take * j, take)],
            rows.at[slot(me, c)],
            a_send.at[d],
            a_recv.at[me],
            peer_place(j, c),
        )
        copy.start()
        sends.append(copy)

    def forward(d):
        j = peer(d)
        region = rows.at[slot(j, c)]
        copy = send(region, region, f_send.at[d], f_recv.at[j], sibling)
        copy.start()
        sends.append(copy)

    forward(0)

    w_all = w_proj_ref[...]
    w_kt = dot(picker(1, True), w_all, NT).astype(BF)
    w_v = dot(w_all, picker(2, False), NN).astype(BF)
    w_qg = jnp.concatenate([dot(w_all, picker(0, False), NN), dot(w_all, picker(3, False), NN)], axis=1).astype(BF)
    s_row = lax.broadcasted_iota(jnp.int32, (24, HEADS), 0)
    s_head = lax.broadcasted_iota(jnp.int32, (24, HEADS), 1)
    w_bias = w_bias_ref[...]
    w_rows = [
        dot(jnp.where(s_row == s_head * ROWS + r, 1.0, 0.0).astype(BF), w_bias, NN).astype(BF) for r in range(ROWS)
    ]

    for d in range(1, n_peer):
        j = peer(d)
        region = rows.at[slot(j, c)]
        send(region, region, a_send.at[d], a_recv.at[j], sibling).wait_recv()
        forward(d)
    for d in range(n_peer):
        j = peer(d)
        region = rows.at[slot(j, other)]
        send(region, region, f_send.at[d], f_recv.at[j], sibling).wait_recv()

    piece = jnp.zeros((24, N), F32)
    for r in range(ROWS):
        piece += dot(w_rows[r], rows[:, r].reshape(N, CH), NT)
    piece = jnp.where(key_ok > 0, piece * ROOT, MASKED)
    y2 = y // 2
    if starting:
        source = lax.rem(z, 2) == c
        own_piece = bias.at[xh, z // 2, xl, y]
        part = lambda k: bias.at[xh, k // 2, xl, y]
        comes = lambda k: jnp.logical_and(lax.rem(k, 2) == c, k != z)
    else:
        source = lax.rem(y, 2) == c
        own_piece = bias.at[xl, y2, xh, z]
        part = lambda k: bias.at[xl, y2, xh, k]
        comes = lambda k: jnp.logical_and(source, k != z)

    def first(w, d):
        region = own_piece.at[WAVES[w]]
        return send(region, region, p_send.at[w, d], p_recv.at[w, z], z_place(d))

    @pl.when(source)
    def _():
        own_piece[...] = piece
        for w in range(len(WAVES)):
            for d in range(1, 8):
                first(w, d).start()

    for r in range(ROWS):
        x_r = rows[:, r].reshape(N, CH)
        k_t[r] = dot(w_kt, x_r, NT).astype(BF)
        v_ext[r, :, :CH] = dot(x_r, w_v, NN).astype(BF)
        v_ext[r, :, CH:] = jnp.ones((N, CH), BF)

    def queries(u, r):
        if starting:
            spots = (4 * u + c, 4 * u + 2 + c)
        else:
            spots = (4 * u + 2 * c, 4 * u + 2 * c + 1)
        x_q = jnp.concatenate([rows[spots[0], r], rows[spots[1], r]], axis=0)
        qg = dot(x_q, w_qg, NN).astype(BF)
        big = dot(expand_ref[...], qg, NN)
        q = (big[:, :CH] * head_ref[...]).reshape(*lead, 24, CH)
        g = (jax.nn.sigmoid(big[:, CH:]) * head_ref[...]).reshape(*lead, 24, CH)
        q_exp[(r, *in_super(u))] = q
        g_exp[(r, *in_super(u))] = g

    if starting:
        lead = (2, 2, 4)
        in_super = lambda u: (u // 2, pl.ds(2 * (u % 2), 2))
    else:
        lead = (2, 8)
        in_super = lambda u: (u // 2, u % 2)

    for r in range(ROWS):
        queries(0, r)
    def first_wait(w):
        for k in range(8):

            @pl.when(comes(k))
            def _():
                region = part(k).at[WAVES[w]]
                send(region, region, p_send.at[w, 0], p_recv.at[w, k], sibling).wait_recv()

    x_args = (x_place(1), x_place(-1), g_send, g_recv)
    y_args = (y_place(1), y_place(-1), g_send, g_recv)
    a1, b1, a2, b2 = [], [], [], []
    for w, rw in enumerate(WAVES):
        base = 16 * w
        if starting:
            a1.append(Ring(
                4, y, lambda k, rw=rw: bias.at[xh, pl.ds(0, 2), xl, k, rw],
                lambda k, rw=rw: (bias.at[xh, 0, xl, k, rw], bias.at[xh, 1, xl, k, rw]), *y_args, base,
            ))
            b1.append(Ring(
                4, x, lambda k, rw=rw: bias.at[k // 2, pl.ds(2, 2), lax.rem(k, 2), y, rw],
                lambda k, rw=rw: (bias.at[k // 2, 2, lax.rem(k, 2), y, rw], bias.at[k // 2, 3, lax.rem(k, 2), y, rw]), *x_args, base + 4,
            ))
            a2.append(Ring(
                4, x, lambda k, rw=rw: bias.at[k // 2, pl.ds(0, 2), lax.rem(k, 2), slice(None), rw],
                lambda k, rw=rw: (bias.at[k // 2, 0, lax.rem(k, 2), slice(None), rw], bias.at[k // 2, 1, lax.rem(k, 2), slice(None), rw]), *x_args, base + 8,
            ))
            b2.append(Ring(
                4, y, lambda k, rw=rw: bias.at[:, pl.ds(2, 2), :, k, rw],
                lambda k, rw=rw: (bias.at[:, 2, :, k, rw], bias.at[:, 3, :, k, rw]), *y_args, base + 12,
            ))
        else:
            has = lambda k: lax.rem(k, 2) == c
            here_only = lambda k: source
            a1.append(Ring(
                4, y, lambda k, rw=rw: bias.at[xl, k // 2, xh, pl.ds(0, 4), rw],
                lambda k, rw=rw: (bias.at[xl, k // 2, xh, pl.ds(0, 2), rw], bias.at[xl, k // 2, xh, pl.ds(2, 2), rw]), *y_args, base, has,
            ))
            b1.append(Ring(
                4, x, lambda k, rw=rw: bias.at[lax.rem(k, 2), y2, k // 2, pl.ds(4, 4), rw],
                lambda k, rw=rw: (
                    bias.at[lax.rem(k, 2), y2, k // 2, pl.ds(4, 2), rw],
                    bias.at[lax.rem(k, 2), y2, k // 2, pl.ds(6, 2), rw],
                ), *x_args, base + 4, here_only,
            ))
            a2.append(Ring(
                4, x, lambda k, rw=rw: bias.at[lax.rem(k, 2), :, k // 2, pl.ds(0, 4), rw],
                lambda k, rw=rw: (
                    bias.at[lax.rem(k, 2), 0, k // 2, pl.ds(0, 4), rw],
                    bias.at[lax.rem(k, 2), 1, k // 2, pl.ds(0, 4), rw],
                ), *x_args, base + 8,
            ))
            b2.append(Ring(
                4, y, lambda k, rw=rw: bias.at[:, k // 2, :, pl.ds(4, 4), rw],
                lambda k, rw=rw: (bias.at[0, k // 2, :, pl.ds(4, 4), rw], bias.at[1, k // 2, :, pl.ds(4, 4), rw]), *y_args, base + 12, has,
            ))

    both = range(len(WAVES))
    def phase_a(w):
        first_wait(w)
        a1[w].start()
        b1[w].start()

    phase_a(0)
    for r in range(ROWS):
        queries(1, r)
    a1[0].advance(1)
    b1[0].advance(1)
    phase_a(1)
    a1[0].advance(2)
    b1[0].advance(2)
    a2[0].start()
    b2[0].start()
    for step in (1, 2):
        a1[1].advance(step)
        b1[1].advance(step)
    a2[1].start()
    b2[1].start()
    for r in range(ROWS):
        queries(2, r)
        queries(3, r)

    if starting:
        line_at = TILE * (8 * xh + z)
        valid = [mask_smem[line_at + ROWS * me + r] for r in range(ROWS)]
    else:
        line_at = TILE * 2 * (4 * xl + y)
        valid = [mask_smem[line_at + TILE * (r // 3) + 3 * me + r % 3] for r in range(ROWS)]
    power = [v.astype(F32) * (INV_ROOT * LOG2E) for v in valid]

    def attend(at):
        pairs = bias[at].reshape(SUB, N)
        for r in range(ROWS):
            t = dot(q_exp[(r, *at)].reshape(SUB, CH).astype(BF), k_t[r], NN) + pairs
            top = jnp.max(t, axis=1, keepdims=True)
            e = jnp.exp2((t - top) * power[r]).astype(BF)
            o = dot(e, v_ext[r], NN)
            gated = g_exp[(r, *at)].reshape(SUB, CH) * (o[:, :CH] / o[:, CH:])
            gat[(r, *at)] = gated.reshape(*q_exp[(r, *at)].shape)

    def collapse(u):
        for r in range(ROWS):
            wide = gat[(r, *in_super(u))].reshape(EXP, CH).astype(BF)
            joined = dot(collapse_ref[...], wide, NN).astype(BF)
            new = dot(joined, w_out_ref[...], NN).astype(BF)
            upd[2 * u, r] = new[:TILE]
            upd[2 * u + 1, r] = new[TILE:]

    back_to = ret.at[pl.ds(take * me, take)]

    def backs(u, at):
        for blk in (0, 1):
            q = 2 * u + blk
            if starting:
                yield q != me, send(upd.at[q], back_to, r_send.at[2 * at + blk], r_recv.at[me], peer_place(q, c))
            else:
                p = 4 * u + 2 * c + blk
                for core in (0, 1):
                    yield jnp.logical_or(p != me, c != core), send(
                        upd.at[q, pl.ds(3 * core, 3)],
                        back_to,
                        r_send.at[4 * at + 2 * blk + core],
                        r_recv.at[me],
                        peer_place(p, core),
                    )

    def give(u, at):
        collapse(u)
        for other_device, copy in backs(u, at):
            pl.when(other_device)(copy.start)

    done = (0, 2, 1, 3) if starting else (2 - 2 * xl, 3 - 2 * xl, 2 * xl, 2 * xl + 1)

    if starting:

        def last(step):
            xc = lax.rem(x + step, 4)
            return (
                (xc // 2, pl.ds(0, 2), lax.rem(xc, 2)),
                (slice(None), pl.ds(2, 2), slice(None), lax.rem(y + step, 4)),
            )

        @pl.loop(0, 3)
        def _(t):
            @pl.when(t == 1)
            def _():
                for w in both:
                    a2[w].advance(1)
                    b2[w].advance(1)

            for spot in last(jnp.where(t == 2, 3, t)):
                attend(spot)

        for w in both:
            a2[w].advance(2)
            b2[w].advance(2)
        attend(last(2)[0])
        give(done[0], 0)
        give(done[1], 1)
        attend(last(2)[1])
    else:

        @pl.loop(0, 8)
        def _(h):
            t = h // 2
            step = jnp.where(t == 3, 2, jnp.where(t == 2, 3, t))
            first_kind = lax.rem(h, 2) == 0
            if not starting:
                first_kind = jnp.where(h < 6, lax.rem(h, 2), 7 - h) == 0
            rings = {1: [], 2: [], 5: [], 6: [], 7: []}
            if starting:
                rings[2] = [(a2, 1), (b2, 1)]
                rings[6] = [(a2, 2), (b2, 2)]
            else:
                rings[1] = [(b2, 1)]
                rings[2] = [(a2, 1)]
                rings[5] = [(b2, 2)]
                rings[7] = [(a2, 2)]
            for when, moves in rings.items():
                if moves:

                    @pl.when(h == when)
                    def _():
                        for ring, move in moves:
                            for w in both:
                                ring[w].advance(move)

            xc = lax.rem(x + step, 4)

            @pl.when(first_kind)
            def _():
                if starting:
                    attend((xc // 2, pl.ds(0, 2), lax.rem(xc, 2)))
                else:
                    attend((lax.rem(xc, 2), slice(None), xc // 2, pl.ds(0, 4)))

            @pl.when(jnp.logical_not(first_kind))
            def _():
                if starting:
                    attend((slice(None), pl.ds(2, 2), slice(None), lax.rem(y + step, 4)))
                else:
                    y_c = jnp.where(t < 2, y2, 1 - y2)
                    attend((lax.rem(t, 2), y_c, slice(None), pl.ds(4, 4)))

            @pl.when(h == 6)
            def _():
                give(done[0], 0)
                give(done[1], 1)

    give(done[2], 2)
    give(done[3], 3)
    if starting:
        back_to[...] = upd[me]
    else:
        mine = lax.rem(me // 2, 2) == c

        @pl.when(mine)
        def _():
            back_to[...] = upd[2 * (me // 4) + lax.rem(me, 2), pl.ds(3 * c, 3)]

    for d in range(n_peer):
        j = peer(d)
        region = ret.at[pl.ds(take * j, take)]
        come = send(region, region, r_send.at[d], r_recv.at[j], sibling)
        if d:
            come.wait_recv()
        elif not starting:
            pl.when(jnp.logical_not(mine))(come.wait_recv)

    def finish():
        for copy in sends:
            copy.wait_send()
        for at, u in enumerate(done):
            for other_device, copy in backs(u, at):
                pl.when(other_device)(copy.wait_send)

        @pl.when(source)
        def _():
            for w in both:
                for d in range(1, 8):
                    first(w, d).wait_send()

        for ring in (*a1, *b1, *a2, *b2):
            ring.finish()

    return finish


class Bag:
    pass


def kernel(
    tile_ref,
    mask_smem,
    mask_ref,
    ps_ref,
    bs_ref,
    os_ref,
    pe_ref,
    be_ref,
    oe_ref,
    es_ref,
    cs_ref,
    ee_ref,
    ce_ref,
    head_ref,
    start_ref,
    end_ref,
    nt_start,
    nt_end,
    rows_start,
    rows_end,
    bias_start,
    bias_end,
    ret_start,
    ret_end,
    k_t,
    v_ext,
    q_exp,
    g_exp,
    gat,
    upd,
    *sems,
):
    at = here()
    xh, z, xl, y, c = (at[a] for a in AXES)
    x = 2 * xh + xl
    narrow_me, wide_me = xl * 4 + y, xh * 8 + z
    partners = [place(at, c=1 - c)]
    for d in range(1, 8):
        j = lax.rem(narrow_me + d, 8)
        partners.append(place(at, xl=j // 4, y=lax.rem(j, 4)))
    for d in range(1, 16):
        j = lax.rem(wide_me + d, 16)
        for core in (c, 1 - c):
            partners.append(place(at, xh=j // 8, z=lax.rem(j, 8), c=core))
    far = lax.rem(x + jnp.where(xl == 0, 3, 1), 4)
    partners.append(place(at, xh=far // 2, xl=lax.rem(far, 2)))
    barrier = pltpu.get_barrier_semaphore()
    for partner in partners:
        pl.semaphore_signal(barrier, inc=1, device_id=partner, device_id_type=pl.DeviceIdType.MESH)

    b = Bag()
    b.k_t, b.v_ext, b.upd = k_t, v_ext, upd
    b.q_exp, b.g_exp, b.gat = q_exp, g_exp, gat
    key_ok = mask_ref[...].reshape(1, N)
    b.given = {
        True: (mask_smem, key_ok, ps_ref, bs_ref, os_ref, es_ref, cs_ref, head_ref),
        False: (mask_smem, key_ok, pe_ref, be_ref, oe_ref, ee_ref, ce_ref, head_ref),
    }
    half = len(sems) // 2

    nt_start[...] = layer_norm(tile_ref[...].astype(F32))
    finish_start = run(
        True, b, lambda: pl.semaphore_wait(barrier, len(partners)), nt_start, rows_start, bias_start, ret_start, sems[:half]
    )
    update = ret_start[...]
    start_ref[...] = update
    normed = layer_norm(tile_ref[...].astype(F32) + update.astype(F32))
    nt_end[...] = jnp.swapaxes(normed.astype(F32), 0, 1).astype(BF)
    finish_start()
    finish_end = run(False, b, lambda: None, nt_end, rows_end, bias_end, ret_end, sems[half:])
    end_ref[...] = jnp.swapaxes(ret_end[...].astype(F32), 0, 1).astype(BF)
    finish_end()


def expansion(starting):
    row = np.arange(EXP)
    if starting:
        blk, slot, r = row // 192, row % 192 // 24, row % 6
        pos = blk * TILE + 6 * slot + r
    else:
        slot, r6 = row // 24, row % 6
        pos = (r6 // 3) * TILE + 3 * slot + r6 % 3
    expand = (pos[:, None] == np.arange(POS)[None, :]).astype(np.float32)
    head = (row // 6 % HEADS)[:, None] == (np.arange(CH) // DIM)[None, :]
    return expand, head.astype(np.float32)


def on_device(pair_act, mask, w_proj_start, w_bias_start, w_out_start, w_proj_end, w_bias_end, w_out_end):
    (e_start, head), (e_end, _) = expansion(True), expansion(False)
    vmem = pl.BlockSpec(memory_space=pltpu.VMEM)
    smem = pl.BlockSpec(memory_space=pltpu.SMEM)
    dma = pltpu.SemaphoreType.DMA
    tile = pltpu.VMEM((TILE, TILE, CH), BF)
    rows = pltpu.VMEM((16, ROWS, TILE, CH), BF)
    wide_rows = pltpu.VMEM((ROWS, 64, 24, CH), F32)
    sems = [dma((16,)) for _ in range(4)] + [dma((2, 8)) for _ in range(2)] + [dma((32,)) for _ in range(2)] + [dma((16,)) for _ in range(2)]
    return pl.pallas_call(
        kernel,
        out_shape=[jax.ShapeDtypeStruct((TILE, TILE, CH), BF)] * 2,
        in_specs=[vmem, smem] + [vmem] * 12,
        out_specs=[vmem, vmem],
        scratch_shapes=[
            tile,
            tile,
            rows,
            rows,
            pltpu.VMEM((2, 4, 2, 4, 24, N), F32),
            pltpu.VMEM((2, 2, 2, 8, 24, N), F32),
            tile,
            tile,
            pltpu.VMEM((ROWS, CH, N), BF),
            pltpu.VMEM((ROWS, N, 2 * CH), BF),
            wide_rows,
            wide_rows,
            wide_rows,
            pltpu.VMEM((8, ROWS, TILE, CH), BF),
        ]
        + sems
        + sems,
        compiler_params=pltpu.CompilerParams(
            collective_id=0, has_side_effects=True, vmem_limit_bytes=56 * 1024 * 1024
        ),
        name="triangle_attention",
    )(
        pair_act,
        mask,
        mask,
        w_proj_start,
        w_bias_start.T,
        w_out_start,
        w_proj_end,
        w_bias_end.T,
        w_out_end,
        jnp.asarray(e_start, BF),
        jnp.asarray(e_start.T, BF),
        jnp.asarray(e_end, BF),
        jnp.asarray(e_end.T, BF),
        jnp.asarray(head, F32),
    )


def solution(mesh):
    split = Mesh(mesh.devices.reshape(SIZES), AXES)
    placed = (P(WIDE, NARROW, None),) + (P(),) * 7
    return jax.shard_map(
        on_device,
        mesh=split,
        in_specs=placed,
        out_specs=(P(WIDE, NARROW, None), P(WIDE, NARROW, None)),
        check_vma=False,
    )
```
